32 devices in a mesh: dp: 8 (over z, core), mp: 4 (over y, x).
Axes of the slice: x: 2, y: 2, z: 4, core: 2. Of those that a mesh axis runs over, the one named last changes fastest.
Arguments:
- prefix_tokens: bfloat16 [6528, 2048], P('dp', 'mp'), may hold values from -6 to 6
- action_tokens: bfloat16 [400, 1024], P('dp', 'mp'), may hold values from -6 to 6
- camera_counts: int32 [8], P('dp'), may hold values from 1 to 3
- text_lengths: int32 [8], P('dp'), may hold values from 1 to 48
- prefix_attn_gain: float32 [2048], P('mp'), may hold values from 0.5 to 1.5
- prefix_query_proj: bfloat16 [2048, 2048], P('dp', 'mp'), may hold values from -0.125 to 0.125
- prefix_kv_proj: bfloat16 [2048, 512], P('dp', 'mp'), may hold values from -0.125 to 0.125
- prefix_out_proj: bfloat16 [2048, 2048], P('mp', 'dp'), may hold values from -2.5 to 2.5
- prefix_ffn_gain: float32 [2048], P('mp'), may hold values from 0.5 to 1.5
- prefix_gate_proj: bfloat16 [2048, 16384], P('dp', 'mp'), may hold values from -0.125 to 0.125
- prefix_up_proj: bfloat16 [2048, 16384], P('dp', 'mp'), may hold values from -0.125 to 0.125
- prefix_down_proj: bfloat16 [16384, 2048], P('mp', 'dp'), may hold values from -0.046875 to 0.046875
- action_attn_gain: float32 [1024], P('mp'), may hold values from 0.5 to 1.5
- action_query_proj: bfloat16 [1024, 2048], P('dp', 'mp'), may hold values from -0.1875 to 0.1875
- action_kv_proj: bfloat16 [1024, 512], P('dp', 'mp'), may hold values from -0.1875 to 0.1875
- action_out_proj: bfloat16 [2048, 1024], P('mp', 'dp'), may hold values from -2.5 to 2.5
- action_ffn_gain: float32 [1024], P('mp'), may hold values from 0.5 to 1.5
- action_gate_proj: bfloat16 [1024, 4096], P('dp', 'mp'), may hold values from -0.1875 to 0.1875
- action_up_proj: bfloat16 [1024, 4096], P('dp', 'mp'), may hold values from -0.1875 to 0.1875
- action_down_proj: bfloat16 [4096, 1024], P('mp', 'dp'), may hold values from -0.09375 to 0.09375
- prefix_cotangent: bfloat16 [6528, 2048], P('dp', 'mp'), may hold values from -6 to 6
- action_cotangent: bfloat16 [400, 1024], P('dp', 'mp'), may hold values from -6 to 6
Outputs:
- prefix_output: float32 [6528, 2048], P('dp', 'mp')
- action_output: float32 [400, 1024], P('dp', 'mp')
- prefix_gradient: float32 [6528, 2048], P('dp', 'mp')
- action_gradient: float32 [400, 1024], P('dp', 'mp')
- grad_prefix_attn_gain: float32 [2048], P('mp')
- grad_prefix_query_proj: float32 [2048, 2048], P('dp', 'mp')
- grad_prefix_kv_proj: float32 [2048, 512], P('dp', 'mp')
- grad_prefix_out_proj: float32 [2048, 2048], P('mp', 'dp')
- grad_prefix_ffn_gain: float32 [2048], P('mp')
- grad_prefix_gate_proj: float32 [2048, 16384], P('dp', 'mp')
- grad_prefix_up_proj: float32 [2048, 16384], P('dp', 'mp')
- grad_prefix_down_proj: float32 [16384, 2048], P('mp', 'dp')
- grad_action_attn_gain: float32 [1024], P('mp')
- grad_action_query_proj: float32 [1024, 2048], P('dp', 'mp')
- grad_action_kv_proj: float32 [1024, 512], P('dp', 'mp')
- grad_action_out_proj: float32 [2048, 1024], P('mp', 'dp')
- grad_action_ffn_gain: float32 [1024], P('mp')
- grad_action_gate_proj: float32 [1024, 4096], P('dp', 'mp')
- grad_action_up_proj: float32 [1024, 4096], P('dp', 'mp')
- grad_action_down_proj: float32 [4096, 1024], P('mp', 'dp')
The draws below stay inside these ranges and needn't reach their ends.
All inputs are finite; a program needn't handle non-finite values.
Results may differ from the reference program's by a relative error of at most 0.02.
Values may be sent and summed in bfloat16 or wider, within the bound.
No kernel may reach another device: no remote copies, remote signals or barrier semaphores. Data moves between devices by JAX's collectives and lax.ppermute only.
A program may use at most 320 MiB of HBM per device.

```python
import jax
import jax.numpy as jnp
from jax import lax

D = 2048
FF = 16384
H = 8
HD = 256
DA = 1024
FFA = 4096
IMG = 256
CAMS = 3
TEXT = 48
A = 50
P_SIZE = 816
EPISODES = 8


def touch_ends(values, own_key, least, largest):
    place = [jax.random.randint(jax.random.fold_in(own_key, axis), (), 0, length) for axis, length in enumerate(values.shape)]
    widest = values.shape.index(max(values.shape))
    next_to = place[:widest] + [(place[widest] + 1) % values.shape[widest]] + place[widest + 1:]
    return values.at[tuple(place)].set(least).at[tuple(next_to)].set(largest)


def block_scale(stream_key, extent, cuts, low, largest):
    level = 1.0
    for dim, shards_of in cuts:
        steps = jax.random.uniform(jax.random.fold_in(jax.random.fold_in(stream_key, 6), dim), (shards_of,), jnp.float32, low / len(cuts), largest / len(cuts))
        level = level * jnp.repeat(jnp.exp(steps), extent[dim] // shards_of).reshape((-1,) + (1,) * (len(extent) - 1 - dim))
    return level


def normal_values(own_key, extent, width, bound, cuts=(), kind=jnp.bfloat16):
    values = jax.random.normal(own_key, extent, jnp.float32) * width
    if len(cuts) > 0:
        values = block_scale(own_key, extent, cuts, -0.22, 0.18) * values
    return jnp.clip(values, min=-bound, max=bound).astype(kind)


def setup_inputs(seed: int = 0) -> dict:
    splits = jax.random.split(jax.random.key(seed), 23)
    return {
        "prefix_tokens": normal_values(splits[0], (EPISODES * P_SIZE, D), 1.0, 6.0, ((0, 8), (1, 4))),
        "action_tokens": normal_values(splits[1], (EPISODES * A, DA), 1.0, 6.0, ((0, 8), (1, 4))),
        "camera_counts": touch_ends(jax.random.randint(splits[2], (EPISODES,), 1, CAMS + 1), jax.random.fold_in(splits[2], 1), 1, CAMS).astype(jnp.int32),
        "text_lengths": touch_ends(jax.random.randint(splits[3], (EPISODES,), 1, TEXT + 1), jax.random.fold_in(splits[3], 1), 1, TEXT).astype(jnp.int32),
        "prefix_attn_gain": jnp.clip(1.0 + 0.1 * jax.random.normal(splits[4], (D,), jnp.float32), 0.5, 1.5),
        "prefix_query_proj": normal_values(splits[5], (D, H * HD), D ** -0.5, 0.125, ((0, 8), (1, 4))),
        "prefix_kv_proj": normal_values(splits[6], (D, 2 * HD), D ** -0.5, 0.125, ((0, 8), (1, 4))),
        "prefix_out_proj": normal_values(splits[7], (H * HD, D), (2 * H * HD // P_SIZE) ** -0.5, 2.5, ((0, 4), (1, 8))),
        "prefix_ffn_gain": jnp.clip(1.0 + 0.1 * jax.random.normal(splits[8], (D,), jnp.float32), 0.5, 1.5),
        "prefix_gate_proj": normal_values(splits[9], (D, FF), D ** -0.5, 0.125, ((0, 8), (1, 4))),
        "prefix_up_proj": normal_values(splits[10], (D, FF), D ** -0.5, 0.125, ((0, 8), (1, 4))),
        "prefix_down_proj": normal_values(splits[11], (FF, D), FF ** -0.5, 0.046875, ((0, 4), (1, 8))),
        "action_attn_gain": jnp.clip(1.0 + 0.1 * jax.random.normal(splits[12], (DA,), jnp.float32), 0.5, 1.5),
        "action_query_proj": normal_values(splits[13], (DA, H * HD), DA ** -0.5, 0.1875, ((0, 8), (1, 4))),
        "action_kv_proj": normal_values(splits[14], (DA, 2 * HD), DA ** -0.5, 0.1875, ((0, 8), (1, 4))),
        "action_out_proj": normal_values(splits[15], (H * HD, DA), (2 * H * HD // P_SIZE) ** -0.5, 2.5, ((0, 4), (1, 8))),
        "action_ffn_gain": jnp.clip(1.0 + 0.1 * jax.random.normal(splits[16], (DA,), jnp.float32), 0.5, 1.5),
        "action_gate_proj": normal_values(splits[17], (DA, FFA), DA ** -0.5, 0.1875, ((0, 8), (1, 4))),
        "action_up_proj": normal_values(splits[18], (DA, FFA), DA ** -0.5, 0.1875, ((0, 8), (1, 4))),
        "action_down_proj": normal_values(splits[19], (FFA, DA), FFA ** -0.5, 0.09375, ((0, 4), (1, 8))),
        "prefix_cotangent": normal_values(splits[20], (EPISODES * P_SIZE, D), 1.0, 6.0, ((0, 8), (1, 4))),
        "action_cotangent": normal_values(splits[21], (EPISODES * A, DA), 1.0, 6.0, ((0, 8), (1, 4))),
    }


EPSILON = 1e-06
MASKED = -1e+30
HIGHEST = lax.Precision.HIGHEST

@jax.custom_vjp
def low(v):
    return lax.optimization_barrier(v.astype(jnp.bfloat16)).astype(jnp.float32)

@jax.custom_vjp
def low_back(v):
    return v

def low_keep(v):
    return (low(v), None)

def low_pass(kept, grad):
    return (grad,)

def back_keep(v):
    return (v, None)

def back_low(kept, grad):
    return (low(grad),)
low.defvjp(low_keep, low_pass)
low_back.defvjp(back_keep, back_low)

def rounded_both(values_in):
    return low_back(low(values_in))

def matmul(matrix, factor):
    return jnp.dot(matrix, factor, precision=HIGHEST)

def normed(inputs, gain_vec):
    inv_rms = lax.rsqrt(lax.optimization_barrier(jnp.mean(inputs * inputs, axis=1, keepdims=True)) + EPSILON)
    return inputs * inv_rms * gain_vec

def attend(query_rows, key_rows, value_rows, key_mask):
    scores = jnp.einsum('qhd,kd->hqk', query_rows, key_rows, precision=HIGHEST) * HD ** (-0.5)
    scores = low_back(scores)
    scores = jnp.where(key_mask[None, None, :], scores, MASKED)
    highest = lax.optimization_barrier(jnp.max(scores, axis=-1, keepdims=True))
    exp_terms = jnp.exp(scores - highest)
    attn_weights = exp_terms / lax.optimization_barrier(jnp.sum(exp_terms, axis=-1, keepdims=True))
    return jnp.einsum('hqk,kd->qhd', low(attn_weights), value_rows, precision=HIGHEST)

def layer_one(prefix, action, key_mask, weights):
    gain_attn_pre, query_pre, keyval_pre, outproj_pre, gain_ffn_pre, gate_pre, upward_pre, downward_pre, gain_attn_act, query_act, keyval_act, outproj_act, gain_ffn_act, gate_act, upward_act, downward_act = weights
    normed_pre = low(normed(prefix, gain_attn_pre))
    normed_act = low(normed(action, gain_attn_act))
    queries_pre = rounded_both(matmul(normed_pre, query_pre)).reshape(P_SIZE, H, HD)
    queries_act = rounded_both(matmul(normed_act, query_act)).reshape(A, H, HD)
    kvrows_pre = rounded_both(matmul(normed_pre, keyval_pre))
    kvrows_act = rounded_both(matmul(normed_act, keyval_act))
    key_all = jnp.concatenate([kvrows_pre[:, :HD], kvrows_act[:, :HD]], axis=0)
    value_all = jnp.concatenate([kvrows_pre[:, HD:], kvrows_act[:, HD:]], axis=0)
    mask_all = jnp.concatenate([key_mask, jnp.ones((A,), jnp.bool_)])
    mixed_pre = rounded_both(attend(queries_pre, kvrows_pre[:, :HD], kvrows_pre[:, HD:], key_mask).reshape(P_SIZE, H * HD))
    mixed_act = rounded_both(attend(queries_act, key_all, value_all, mask_all).reshape(A, H * HD))
    middle_pre = prefix + low_back(matmul(mixed_pre, outproj_pre))
    middle_act = action + low_back(matmul(mixed_act, outproj_act))
    normed2_pre = low(normed(middle_pre, gain_ffn_pre))
    normed2_act = low(normed(middle_act, gain_ffn_act))
    gate_val_pre = low_back(matmul(normed2_pre, gate_pre))
    upval_pre = low_back(matmul(normed2_pre, upward_pre))
    gate_val_act = low_back(matmul(normed2_act, gate_act))
    upval_act = low_back(matmul(normed2_act, upward_act))
    hidden_pre = low(jax.nn.gelu(gate_val_pre, approximate=True) * upval_pre)
    hidden_act = low(jax.nn.gelu(gate_val_act, approximate=True) * upval_act)
    output_pre = middle_pre + matmul(hidden_pre, downward_pre)
    output_act = middle_act + matmul(hidden_act, downward_act)
    return (output_pre, output_act)

def reference(prefix_tokens, action_tokens, camera_counts, text_lengths, prefix_attn_gain, prefix_query_proj, prefix_kv_proj, prefix_out_proj, prefix_ffn_gain, prefix_gate_proj, prefix_up_proj, prefix_down_proj, action_attn_gain, action_query_proj, action_kv_proj, action_out_proj, action_ffn_gain, action_gate_proj, action_up_proj, action_down_proj, prefix_cotangent, action_cotangent):
    episodes = camera_counts.shape[0]
    weights = tuple((entry.astype(jnp.float32) for entry in (prefix_attn_gain, prefix_query_proj, prefix_kv_proj, prefix_out_proj, prefix_ffn_gain, prefix_gate_proj, prefix_up_proj, prefix_down_proj, action_attn_gain, action_query_proj, action_kv_proj, action_out_proj, action_ffn_gain, action_gate_proj, action_up_proj, action_down_proj)))
    prefix = prefix_tokens.astype(jnp.float32).reshape(episodes, P_SIZE, D)
    action = action_tokens.astype(jnp.float32).reshape(episodes, A, DA)
    position = jnp.arange(P_SIZE, dtype=jnp.int32)[None, :]
    image_end = camera_counts[:, None] * IMG
    text_start = CAMS * IMG
    key_mask = (position < image_end) | (position >= text_start) & (position < text_start + text_lengths[:, None])
    checked = jax.checkpoint(layer_one)

    def forward(prefix_in, action_in, weights_in):
        return lax.map(lambda triple: checked(triple[0], triple[1], triple[2], weights_in), (prefix_in, action_in, key_mask))
    (output_pre, output_act), pullback = jax.vjp(forward, prefix, action, weights)
    grad_pre, grad_act, grads = pullback((prefix_cotangent.astype(jnp.float32).reshape(episodes, P_SIZE, D), action_cotangent.astype(jnp.float32).reshape(episodes, A, DA)))
    return (output_pre.reshape(episodes * P_SIZE, D), output_act.reshape(episodes * A, DA), grad_pre.reshape(episodes * P_SIZE, D), grad_act.reshape(episodes * A, DA), grads[0], grads[1], grads[2], grads[3], grads[4], grads[5], grads[6], grads[7], grads[8], grads[9], grads[10], grads[11], grads[12], grads[13], grads[14], grads[15])
```

```python
import jax
import jax.numpy as jnp
from jax import lax
from jax.sharding import PartitionSpec as P

HD = 256
IMG = 256
CAMS = 3
EPSILON = 1e-06
MASKED = -1e30
BF = jnp.bfloat16
F32 = jnp.float32


def mm(a, b):
    return jnp.dot(a, b, preferred_element_type=F32)


def mm_tn(a, b):
    return lax.dot_general(a, b, (((0,), (0,)), ((), ())), preferred_element_type=F32)


def mm_nt(a, b):
    return lax.dot_general(a, b, (((1,), (1,)), ((), ())), preferred_element_type=F32)


def pad_rows(a, rows):
    return jnp.pad(a, ((0, rows - a.shape[0]), (0, 0)))


def swap(a, axis, size, step):
    return lax.ppermute(a, axis, [(i, i ^ step) for i in range(size)])


def exchange(a, axis):
    return lax.all_to_all(a, axis, 0, 0, tiled=True)


def copies(a, k):
    return jnp.broadcast_to(a[None], (k,) + a.shape)


def spread_blocks(block, k):
    if k == 4:
        half = block.shape[0] // 2
        first = swap(block, "mp", k, 1)
        second = swap(block, "mp", k, 2)
        low = swap(second[:half], "mp", k, 1)
        high = swap(first[half:], "mp", k, 2)
        return [block, first, second, jnp.concatenate([low, high], axis=0)]
    return [block] + [swap(block, "mp", k, s) for s in range(1, k)]


def collect_blocks(parts, k):
    total = parts[0].astype(F32)
    if k == 4:
        half = parts[0].shape[0] // 2
        low = swap(parts[3][:half], "mp", k, 1)
        high = swap(parts[3][half:], "mp", k, 2)
        first_low = swap(parts[1][:half], "mp", k, 1)
        second_high = swap(parts[2][half:], "mp", k, 2)
        second_low = swap(
            (parts[2][:half].astype(F32) + low.astype(F32)).astype(BF), "mp", k, 2
        )
        first_high = swap(
            (parts[1][half:].astype(F32) + high.astype(F32)).astype(BF), "mp", k, 1
        )
        lower = total[:half] + first_low.astype(F32) + second_low.astype(F32)
        upper = total[half:] + first_high.astype(F32) + second_high.astype(F32)
        return jnp.concatenate([lower.astype(BF), upper.astype(BF)], axis=0)
    for s in range(1, k):
        total = total + swap(parts[s], "mp", k, s).astype(F32)
    return total.astype(BF)


def inverse_rms(x):
    return lax.rsqrt(jnp.mean(x * x, axis=1, keepdims=True) + EPSILON)


def norm_back(grad, x, inv, gain):
    inner = jnp.sum(grad * gain * x, axis=1, keepdims=True)
    back = inv * gain * grad - x * inv**3 * inner / x.shape[1]
    return back, jnp.sum(grad * x * inv, axis=0)


def scores_of(queries, keys, mask):
    scores = jnp.einsum("qhd,kd->hqk", queries, keys, preferred_element_type=F32) * HD ** (-0.5)
    return jnp.where(mask[None, None, :], scores, MASKED)


def attend(queries, keys, values, mask):
    scores = scores_of(queries, keys, mask)
    highest = jnp.max(scores, axis=-1, keepdims=True)
    terms = jnp.exp(scores - highest)
    totals = jnp.sum(terms, axis=-1, keepdims=True)
    low = (terms / totals).astype(BF)
    mixed = jnp.einsum("hqk,kd->qhd", low, values, preferred_element_type=F32)
    return mixed.astype(BF), highest + jnp.log(totals)


def attend_back(queries, keys, values, mask, log_totals, grad_mixed):
    weights = jnp.exp(scores_of(queries, keys, mask) - log_totals)
    grad_attn = jnp.einsum("qhd,kd->hqk", grad_mixed, values, preferred_element_type=F32)
    inner = jnp.sum(weights * grad_attn, axis=-1, keepdims=True)
    grad_scores = (weights * (grad_attn - inner)).astype(BF)
    factor = HD ** (-0.5)
    gq = jnp.einsum("hqk,kd->qhd", grad_scores, keys, preferred_element_type=F32) * factor
    gk = jnp.einsum("hqk,qhd->kd", grad_scores, queries, preferred_element_type=F32) * factor
    gv = jnp.einsum("hqk,qhd->kd", weights.astype(BF), grad_mixed, preferred_element_type=F32)
    return gq, gk, gv


def gelu_both(gate, up, grad_hidden):
    product, pullback = jax.vjp(
        lambda a, b: jax.nn.gelu(a, approximate=True) * b, gate, up
    )
    grad_gate, grad_up = pullback(grad_hidden)
    return product.astype(BF), jnp.concatenate([grad_gate, grad_up], axis=1).astype(BF)


def unit_blocks(gate, up, down, n):
    depth, units = gate.shape[0], gate.shape[1] // n
    gate = gate.reshape(depth, n, units).transpose(1, 0, 2)
    up = up.reshape(depth, n, units).transpose(1, 0, 2)
    down = down.reshape(n, units, depth).transpose(0, 2, 1)
    return jnp.concatenate([gate, up], axis=2), down


def unblock(gate_up, down):
    n, depth, units = down.shape
    gate = gate_up[:, :, :units].transpose(1, 0, 2).reshape(depth, n * units)
    up = gate_up[:, :, units:].transpose(1, 0, 2).reshape(depth, n * units)
    down = down.transpose(0, 2, 1).reshape(n * units, depth)
    return gate.astype(F32), up.astype(F32), down.astype(F32)


def solution(mesh):
    n, k = mesh.shape["dp"], mesh.shape["mp"]

    def per_device(
        prefix_tokens,
        action_tokens,
        camera_counts,
        text_lengths,
        prefix_attn_gain,
        prefix_query_proj,
        prefix_kv_proj,
        prefix_out_proj,
        prefix_ffn_gain,
        prefix_gate_proj,
        prefix_up_proj,
        prefix_down_proj,
        action_attn_gain,
        action_query_proj,
        action_kv_proj,
        action_out_proj,
        action_ffn_gain,
        action_gate_proj,
        action_up_proj,
        action_down_proj,
        prefix_cotangent,
        action_cotangent,
    ):
        mine = lax.axis_index("mp")
        rows, wide = prefix_tokens.shape
        arows, awide = action_tokens.shape
        block = -(-rows // (16 * k)) * 16
        padded = block * k
        apad = -(-arows // 64) * 64
        width, awidth = wide * k, awide * k
        fold = apad * awidth // width
        heads = prefix_query_proj.shape[1] // HD
        qcols = heads * HD
        kvcols = prefix_kv_proj.shape[1]
        depth, adepth = prefix_query_proj.shape[0], action_query_proj.shape[0]

        with jax.named_scope("attention_weights"):
            qkv_pre = jnp.concatenate([prefix_query_proj, prefix_kv_proj], axis=1)
            qkv_act = jnp.concatenate([action_query_proj, action_kv_proj], axis=1)
            out_local = jnp.concatenate([prefix_out_proj.T, action_out_proj.T], axis=0)
            wqkv_pre = lax.all_gather(qkv_pre, "dp", axis=0, tiled=True)
            rest = jnp.concatenate(
                [out_local, jnp.pad(qkv_act, ((0, 0), (0, 0)))[:, :qcols]], axis=0
            )
            rest = lax.all_gather(rest, "dp", axis=0).reshape(n, depth + 2 * adepth, qcols)
            wkv_act = lax.all_gather(qkv_act[:, qcols:], "dp", axis=0, tiled=True)
            wout_pre = rest[:, :depth].reshape(n * depth, qcols)
            wout_act = rest[:, depth : depth + adepth].reshape(n * adepth, qcols)
            wq_act = rest[:, depth + adepth :].reshape(n * adepth, qcols)

        with jax.named_scope("token_features"):
            gains = jnp.concatenate(
                [prefix_attn_gain, prefix_ffn_gain, action_attn_gain, action_ffn_gain]
            )[None]
            gains = exchange(copies(gains, k), "mp")[:, 0]
            gain_pre = gains[:, :wide].reshape(1, width)
            gain2_pre = gains[:, wide : 2 * wide].reshape(1, width)
            gain_act = gains[:, 2 * wide : 2 * wide + awide].reshape(1, awidth)
            gain2_act = gains[:, 2 * wide + awide :].reshape(1, awidth)
            x_act = pad_rows(action_tokens, apad)
            x_all = jnp.concatenate(
                [pad_rows(prefix_tokens, padded), x_act.reshape(-1, wide)], axis=0
            )
            x_all = exchange(copies(x_all, k), "mp")
            x_pre = x_all[:, :padded].transpose(1, 0, 2).reshape(padded, width).astype(F32)
            x_act = (
                x_all[:, padded:]
                .reshape(k, apad, awide)
                .transpose(1, 0, 2)
                .reshape(apad, awidth)
                .astype(F32)
            )

        with jax.named_scope("cotangents"):
            g_act = pad_rows(action_cotangent, apad)
            g_all = jnp.concatenate(
                [
                    pad_rows(prefix_cotangent, padded).reshape(k, block, wide),
                    copies(g_act.reshape(-1, wide), k),
                ],
                axis=1,
            )
            g_all = exchange(g_all, "mp")
            g_pre = g_all[:, :block].transpose(1, 0, 2).reshape(block, width)
            g_act = (
                g_all[:, block:].reshape(k, apad, awide).transpose(1, 0, 2).reshape(apad, awidth)
            )
            gall_pre = lax.all_gather(g_pre, "dp", axis=0, tiled=True)
            gall_act = lax.all_gather(g_act, "dp", axis=0, tiled=True)

        with jax.named_scope("unit_weights"):
            gu_local, dt_local = unit_blocks(prefix_gate_proj, prefix_up_proj, prefix_down_proj, n)
            units = dt_local.shape[2]
            dt_own = exchange(dt_local, "dp").reshape(width, units)
            gu_own = exchange(gu_local, "dp").reshape(width, 2 * units)
            dts = spread_blocks(dt_own, k)
            gus = spread_blocks(gu_own, k)
            gu_act, dt_act = unit_blocks(action_gate_proj, action_up_proj, action_down_proj, n)
            aunits = dt_act.shape[2]
            w_act = exchange(jnp.concatenate([gu_act, dt_act], axis=2), "dp")
            w_act = w_act.reshape(awidth, 3 * aunits)
            gu_act, dt_act = w_act[:, : 2 * aunits], w_act[:, 2 * aunits :]

        with jax.named_scope("attention"):
            mask_pre = jnp.arange(padded, dtype=jnp.int32)
            text = CAMS * IMG
            mask_pre = (mask_pre < camera_counts[0] * IMG) | (
                (mask_pre >= text) & (mask_pre < text + text_lengths[0])
            )
            mask_all = jnp.concatenate([mask_pre, jnp.arange(apad) < arows])
            inv_pre, inv_act = inverse_rms(x_pre), inverse_rms(x_act)
            normed_pre = (x_pre * inv_pre * gain_pre).astype(BF)
            normed_act = (x_act * inv_act * gain_act).astype(BF)
            qkv_p = mm(normed_pre, wqkv_pre).astype(BF)
            q_act = mm(normed_act, wq_act).astype(BF)
            kv_a = mm(normed_act, wkv_act).astype(BF)
            kv = jnp.concatenate([qkv_p[:, qcols:], kv_a], axis=0)
            kv = exchange(copies(kv, k), "mp").transpose(1, 0, 2).reshape(padded + apad, k * kvcols)
            keys, values = kv[:, :HD], kv[:, HD:]
            q_pre = qkv_p[:, :qcols].reshape(padded, heads, HD)
            q_act = q_act.reshape(apad, heads, HD)
            mixed_pre, log_pre = attend(q_pre, keys[:padded], values[:padded], mask_pre)
            mixed_act, log_act = attend(q_act, keys, values, mask_all)
            mixed_pre = mixed_pre.reshape(padded, qcols)
            mixed_act = mixed_act.reshape(apad, qcols)
            branch_pre = mm_nt(mixed_pre, wout_pre).astype(BF).reshape(k, block, width)
            branch_act = mm_nt(mixed_act, wout_act).astype(BF).reshape(fold, width)
            branch = exchange(
                jnp.concatenate([branch_pre, copies(branch_act, k)], axis=1), "mp"
            ).astype(F32)
            branch = jnp.sum(branch, axis=0)
            xrow_pre = lax.dynamic_slice_in_dim(x_pre, mine * block, block, 0)
            middle_pre = xrow_pre + branch[:block]
            middle_act = x_act + branch[block:].reshape(apad, awidth)
            inv2_pre, inv2_act = inverse_rms(middle_pre), inverse_rms(middle_act)
            normed2_pre = (middle_pre * inv2_pre * gain2_pre).astype(BF)
            normed2_act = (middle_act * inv2_act * gain2_act).astype(BF)
            nall_pre = lax.all_gather(normed2_pre, "dp", axis=0, tiled=True)
            nall_act = lax.all_gather(normed2_act, "dp", axis=0, tiled=True)

        with jax.named_scope("geglu"):
            hiddens, grads = [], []
            for gu, dt in zip(gus, dts):
                grad_hidden = mm(gall_pre, dt)
                both = mm(nall_pre, gu)
                hidden, grad = gelu_both(both[:, :units], both[:, units:], grad_hidden)
                hiddens.append(hidden)
                grads.append(grad)
            gn2 = sum(mm_nt(grad, gu) for grad, gu in zip(grads, gus)).astype(BF)
            gn2 = lax.psum_scatter(gn2, "dp", scatter_dimension=0, tiled=True)
            gw_dt = [mm_tn(gall_pre, hidden).astype(BF) for hidden in hiddens]
            gw_gu = [mm_tn(nall_pre, grad).astype(BF) for grad in grads]
            ffn = sum(mm_nt(hidden, dt) for hidden, dt in zip(hiddens, dts)).astype(BF)
            ffn = lax.psum_scatter(ffn, "dp", scatter_dimension=0, tiled=True)
            dgrad = exchange(collect_blocks(gw_dt, k).reshape(n, depth, units), "dp")
            gugrad = exchange(collect_blocks(gw_gu, k).reshape(n, depth, 2 * units), "dp")

            both = mm(nall_act, gu_act)
            hidden, grad = gelu_both(both[:, :aunits], both[:, aunits:], mm(gall_act, dt_act))
            part = jnp.concatenate([mm_nt(hidden, dt_act), mm_nt(grad, gu_act)], axis=1).astype(BF)
            gw_act = jnp.concatenate([mm_tn(nall_act, grad), mm_tn(gall_act, hidden)], axis=1)
            gw_act = exchange(gw_act.astype(BF).reshape(n, adepth, 3 * aunits), "dp")
            part = lax.psum_scatter(part, "dp", scatter_dimension=0, tiled=True)
            part = jnp.concatenate(
                [
                    part[:, :awidth].reshape(apad, k, awide).transpose(1, 0, 2),
                    copies(part[:, awidth:], k),
                ],
                axis=2,
            )
            part = jnp.sum(exchange(part, "mp").astype(F32), axis=0)
            output_act = (
                lax.dynamic_slice_in_dim(middle_act, mine * awide, awide, 1) + part[:, :awide]
            )[:arows]
            gn2_act = part[:, awide:]
            out_pre = (middle_pre + ffn.astype(F32)).astype(BF)
            out_pre = exchange(out_pre.reshape(block, k, wide).transpose(1, 0, 2), "mp")
            output_pre = out_pre.reshape(padded, wide)[:rows].astype(F32)

        with jax.named_scope("middle_norm"):
            back2_pre, gg2_pre = norm_back(gn2.astype(F32), middle_pre, inv2_pre, gain2_pre)
            back2_act, gg2_act = norm_back(gn2_act, middle_act, inv2_act, gain2_act)
            resid_pre = g_pre.astype(F32) + back2_pre
            resid_act = g_act.astype(F32) + back2_act
            gb_pre = exchange(copies(resid_pre.astype(BF), k), "mp").reshape(padded, width)
            gb_act = resid_act.astype(BF)

        with jax.named_scope("attention_back"):
            gm_pre = mm(gb_pre, wout_pre).astype(BF).reshape(padded, heads, HD)
            gm_act = mm(gb_act, wout_act).astype(BF).reshape(apad, heads, HD)
            gq_pre, gk_pre, gv_pre = attend_back(
                q_pre, keys[:padded], values[:padded], mask_pre, log_pre, gm_pre
            )
            gq_act, gk_all, gv_all = attend_back(q_act, keys, values, mask_all, log_act, gm_act)
            gk = jnp.concatenate([gk_pre + gk_all[:padded], gk_all[padded:]], axis=0)
            gv = jnp.concatenate([gv_pre + gv_all[:padded], gv_all[padded:]], axis=0)
            gkv = jnp.concatenate([gk, gv], axis=1).astype(BF)
            gkv = exchange(gkv.reshape(padded + apad, k, kvcols).transpose(1, 0, 2), "mp")
            gkv = jnp.sum(gkv.astype(F32), axis=0).astype(BF)
            gq_pre = gq_pre.reshape(padded, qcols).astype(BF)
            gq_act = gq_act.reshape(apad, qcols).astype(BF)
            gqkv_pre = jnp.concatenate([gq_pre, gkv[:padded]], axis=1)
            gqkv_act = jnp.concatenate([gq_act, gkv[padded:]], axis=1)
            gn_pre = mm_nt(gqkv_pre, wqkv_pre).astype(BF).reshape(k, block, width)
            gn_act = mm_nt(gq_act, wq_act) + mm_nt(gkv[padded:], wkv_act)
            gn = jnp.concatenate(
                [gn_pre, copies(gn_act.astype(BF).reshape(fold, width), k)], axis=1
            )
            gn = jnp.sum(exchange(gn, "mp").astype(F32), axis=0)
            invrow = lax.dynamic_slice_in_dim(inv_pre, mine * block, block, 0)
            back_pre, gg_pre = norm_back(gn[:block], xrow_pre, invrow, gain_pre)
            back_act, gg_act = norm_back(
                gn[block:].reshape(apad, awidth), x_act, inv_act, gain_act
            )
            in_pre = (resid_pre + back_pre).astype(BF)
            in_pre = exchange(in_pre.reshape(block, k, wide).transpose(1, 0, 2), "mp")
            in_pre = in_pre.reshape(padded, wide)[:rows].astype(F32)
            in_act = lax.dynamic_slice_in_dim(resid_act + back_act, mine * awide, awide, 1)[:arows]

        with jax.named_scope("attention_weight_grads"):
            go_pre = mm_tn(gb_pre, mixed_pre).astype(BF).reshape(n, depth, qcols)
            go_act = mm_tn(gb_act, mixed_act).astype(BF).reshape(n, adepth, qcols)
            go = jnp.concatenate([go_pre, go_act], axis=1).reshape(-1, qcols)
            go = lax.psum_scatter(go, "dp", scatter_dimension=0, tiled=True).astype(F32)
            gw_pre = mm_tn(normed_pre, gqkv_pre).astype(BF).reshape(n, depth, -1)
            gw_a = mm_tn(normed_act, gqkv_act).astype(BF).reshape(n, adepth, -1)
            gw = jnp.concatenate([gw_pre, gw_a], axis=1).reshape(-1, qcols + kvcols)
            gw = lax.psum_scatter(gw, "dp", scatter_dimension=0, tiled=True).astype(F32)

        with jax.named_scope("gain_grads"):
            once = (mine == 0).astype(F32)
            gg = jnp.concatenate([gg_pre, gg2_pre, gg_act * once, gg2_act * once])
            gg = lax.psum(gg, ("dp", "mp"))
            gg_pre = lax.dynamic_slice_in_dim(gg, mine * wide, wide)
            gg2_pre = lax.dynamic_slice_in_dim(gg, width + mine * wide, wide)
            gg_act = lax.dynamic_slice_in_dim(gg, 2 * width + mine * awide, awide)
            gg2_act = lax.dynamic_slice_in_dim(gg, 2 * width + awidth + mine * awide, awide)

        with jax.named_scope("unit_weight_grads"):
            gate_pre, up_pre, down_pre = unblock(gugrad, dgrad)
            gate_act, up_act, down_act = unblock(gw_act[:, :, : 2 * aunits], gw_act[:, :, 2 * aunits :])
        return (
            output_pre,
            output_act,
            in_pre,
            in_act,
            gg_pre,
            gw[:depth, :qcols],
            gw[:depth, qcols:],
            go[:depth].T,
            gg2_pre,
            gate_pre,
            up_pre,
            down_pre,
            gg_act,
            gw[depth:, :qcols],
            gw[depth:, qcols:],
            go[depth:].T,
            gg2_act,
            gate_act,
            up_act,
            down_act,
        )

    split, rowsplit, whole = P("dp", "mp"), P("mp", "dp"), P("mp")
    weights = (whole, split, split, rowsplit, whole, split, split, rowsplit)
    return jax.shard_map(
        per_device,
        mesh=mesh,
        in_specs=(split, split, P("dp"), P("dp")) + weights + weights + (split, split),
        out_specs=(split, split, split, split) + weights + weights,
        check_vma=False,
    )
```

```python
import functools

import jax
import jax.numpy as jnp
from jax import lax
from jax.experimental import pallas as pl
from jax.experimental.pallas import tpu as pltpu
from jax.sharding import PartitionSpec as P

HD = 256
IMG = 256
CAMS = 3
EPSILON = 1e-06
MASKED = -1e30
BF = jnp.bfloat16
F32 = jnp.float32
SLOPE = 0.7978845608028654
CUBE = 0.044715
VMEM = 56 * 2**20
BRIEF = pl.CostEstimate(flops=1, bytes_accessed=1, transcendentals=0)


def dot(a, b, over_a, over_b):
    return lax.dot_general(a, b, (((over_a,), (over_b,)), ((), ())), preferred_element_type=F32)


def mm(a, b):
    return dot(a, b, 1, 0)


def mm_tn(a, b):
    return dot(a, b, 0, 0)


def mm_nt(a, b):
    return dot(a, b, 1, 1)


def gelu_parts(gate, up, grad_hidden):
    square = gate * gate
    tanh = jnp.tanh(SLOPE * gate * (1.0 + CUBE * square))
    half = 0.5 * (1.0 + tanh)
    act = gate * half
    slope = half + 0.5 * gate * (1.0 - tanh * tanh) * (SLOPE * (1.0 + 3.0 * CUBE * square))
    return act * up, grad_hidden * up * slope, grad_hidden * act


def geglu_kernel(n_ref, g_ref, gate_up_ref, down_ref, hidden_ref, grad_ref):
    units = down_ref.shape[1]
    rows = n_ref.shape[0] * n_ref.shape[1]
    width = n_ref.shape[2]
    both = mm(n_ref[...].reshape(rows, width), gate_up_ref[...])
    grad_hidden = mm(g_ref[...].reshape(rows, width), down_ref[...])
    hidden, grad_gate, grad_up = gelu_parts(both[:, :units], both[:, units:], grad_hidden)
    hidden_ref[...] = hidden.astype(BF)
    grad_ref[:, :units] = grad_gate.astype(BF)
    grad_ref[:, units:] = grad_up.astype(BF)


def geglu(normed, cots, weights, block, step=2):
    n, _, width = normed.shape
    units = weights.shape[1] // 3
    rows = step * block
    return pl.pallas_call(
        geglu_kernel,
        grid=(n // step,),
        in_specs=[
            pl.BlockSpec((step, block, width), lambda i: (i, 0, 0)),
            pl.BlockSpec((step, block, width), lambda i: (i, 0, 0)),
            pl.BlockSpec((width, 2 * units), lambda i: (0, 0)),
            pl.BlockSpec((width, units), lambda i: (0, 2)),
        ],
        out_specs=[
            pl.BlockSpec((rows, units), lambda i: (i, 0)),
            pl.BlockSpec((rows, 2 * units), lambda i: (i, 0)),
        ],
        out_shape=[
            jax.ShapeDtypeStruct((n * block, units), BF),
            jax.ShapeDtypeStruct((n * block, 2 * units), BF),
        ],
        compiler_params=pltpu.CompilerParams(vmem_limit_bytes=VMEM),
        cost_estimate=BRIEF,
        name="geglu",
    )(normed, cots, weights, weights)


def contract_kernel(count, *refs):
    out = refs[-1]
    total = mm_nt(refs[0][...], refs[count][...])
    for s in range(1, count):
        total += mm_nt(refs[s][...], refs[count + s][...])
    if len(refs) > 2 * count + 1:
        total += refs[2 * count][...]
    out[...] = total.astype(out.dtype)


def contract(parts, weights, column, tile, cols, base=None, kind=BF):
    count, rows = len(parts), parts[0].shape[0]
    width = weights[0].shape[0]
    bases = [] if base is None else [base]
    return pl.pallas_call(
        functools.partial(contract_kernel, count),
        grid=(width // cols, rows // tile),
        in_specs=[pl.BlockSpec((tile, part.shape[1]), lambda j, i: (i, 0)) for part in parts]
        + [pl.BlockSpec((cols, part.shape[1]), lambda j, i: (j, column)) for part in parts]
        + [pl.BlockSpec((tile, cols), lambda j, i: (i, j))] * len(bases),
        out_specs=pl.BlockSpec((tile, cols), lambda j, i: (i, j)),
        out_shape=jax.ShapeDtypeStruct((rows, width), kind),
        compiler_params=pltpu.CompilerParams(vmem_limit_bytes=VMEM),
        cost_estimate=BRIEF,
        name="contract",
    )(*parts, *weights, *bases)


def weight_grad_kernel(n_ref, g_ref, grad_ref, hidden_ref, out_ref):
    rows, cols = n_ref.shape[0] * n_ref.shape[1], n_ref.shape[2]
    units = hidden_ref.shape[1]
    out_ref[:, : 2 * units] = mm_tn(n_ref[...].reshape(rows, cols), grad_ref[...]).astype(BF)
    out_ref[:, 2 * units :] = mm_tn(g_ref[...].reshape(rows, cols), hidden_ref[...]).astype(BF)


def weight_grad(normed, cots, grad, hidden, block, cols=512):
    n, _, width = normed.shape
    units = hidden.shape[1]
    rows = n * block
    return pl.pallas_call(
        weight_grad_kernel,
        grid=(width // cols,),
        in_specs=[
            pl.BlockSpec((n, block, cols), lambda i: (0, 0, i)),
            pl.BlockSpec((n, block, cols), lambda i: (0, 0, i)),
            pl.BlockSpec((rows, 2 * units), lambda i: (0, 0)),
            pl.BlockSpec((rows, units), lambda i: (0, 0)),
        ],
        out_specs=pl.BlockSpec((cols, 3 * units), lambda i: (i, 0)),
        out_shape=jax.ShapeDtypeStruct((width, 3 * units), BF),
        compiler_params=pltpu.CompilerParams(vmem_limit_bytes=VMEM),
        cost_estimate=BRIEF,
        name="weight_grad",
    )(normed, cots, grad, hidden)


def pad_rows(a, rows):
    return jnp.pad(a, ((0, rows - a.shape[0]), (0, 0)))


def swap(a, axis, size, step):
    return lax.ppermute(a, axis, [(i, i ^ step) for i in range(size)])


def exchange(a):
    return lax.all_to_all(a, "dp", 0, 0, tiled=True)


def everyones(a, k):
    return [a] + [swap(a, "mp", k, s) for s in range(1, k)]


def placed(parts, mine, axis):
    size = parts[0].shape[axis]
    shape = list(parts[0].shape)
    shape[axis] *= len(parts)
    whole = jnp.zeros(shape, parts[0].dtype)
    for s, part in enumerate(parts):
        whole = lax.dynamic_update_slice_in_dim(whole, part, (mine ^ s) * size, axis)
    return whole


def handed(a, mine, k, axis):
    size = a.shape[axis] // k
    cut = [lax.dynamic_slice_in_dim(a, (mine ^ s) * size, size, axis) for s in range(k)]
    return [cut[0]] + [swap(cut[s], "mp", k, s) for s in range(1, k)]


def total(parts):
    return sum(part.astype(F32) for part in parts)


def butterfly_sum(a, n):
    step = 1
    while step < n:
        a = a + swap(a, "dp", n, step)
        step *= 2
    return a


class Halving:
    def __init__(self, a, n, me):
        self.a, self.n, self.me, self.step = a, n, me, 1
        self.send()

    def send(self):
        if self.step == self.n:
            return
        a = self.a
        pairs = a.reshape((a.shape[0] // 2, 2) + a.shape[1:])
        bit = (self.me // self.step) % 2
        self.keep = lax.dynamic_index_in_dim(pairs, bit, 1, keepdims=False)
        send = lax.dynamic_index_in_dim(pairs, 1 - bit, 1, keepdims=False)
        self.got = swap(send, "dp", self.n, self.step)

    def take(self, order):
        if self.step == self.n:
            return
        self.a = (self.keep.astype(F32) + order(self.got).astype(F32)).astype(BF)
        self.step *= 2
        self.send()

    def result(self, order):
        while self.step < self.n:
            self.take(order)
        return self.a[0]


class Spread:
    def __init__(self, block, k):
        self.k = k
        if k == 4:
            self.blocks = [block, swap(block, "mp", k, 1), swap(block, "mp", k, 2)]
        else:
            self.blocks = everyones(block, k)

    def arrive(self, order):
        self.blocks[1:] = order(*self.blocks[1:])
        if self.k == 4:
            half = self.blocks[0].shape[0] // 2
            self.low = swap(self.blocks[2][:half], "mp", 4, 1)
            self.high = swap(self.blocks[1][half:], "mp", 4, 2)

    def last(self, order):
        if self.k == 4:
            self.blocks.append(order(jnp.concatenate(order(self.low, self.high), axis=0)))


class Collect:
    def __init__(self, k):
        self.k, self.parts, self.got = k, {}, {}

    def put(self, s, part):
        self.parts[s] = part
        half = part.shape[0] // 2
        if self.k != 4:
            if s:
                self.got[s] = swap(part, "mp", self.k, s)
        elif s == 3:
            self.low = swap(part[:half], "mp", 4, 1)
            self.high = swap(part[half:], "mp", 4, 2)
        elif s == 1:
            self.got["first_low"] = swap(part[:half], "mp", 4, 1)
        elif s == 2:
            self.got["second_high"] = swap(part[half:], "mp", 4, 2)

    def receive(self, order, *names):
        for name in names:
            if name in self.got:
                self.got[name] = order(self.got[name])

    def far(self, order):
        if self.k == 4:
            self.low, self.high = order(self.low, self.high)

    def near(self, order):
        if self.k == 4:
            half = self.low.shape[0]
            low, high = order(
                total([self.parts[2][:half], self.low]).astype(BF),
                total([self.parts[1][half:], self.high]).astype(BF),
            )
            self.got["second_low"] = swap(low, "mp", 4, 2)
            self.got["first_high"] = swap(high, "mp", 4, 1)

    def result(self, order):
        own, got = self.parts[0], self.got
        if self.k != 4:
            return order(total([own, *order(*got.values())]).astype(BF))
        self.receive(order, "first_low", "second_high", "second_low", "first_high")
        half = self.low.shape[0]
        lower = total([own[:half], got["first_low"], got["second_low"]]).astype(BF)
        upper = total([own[half:], got["second_high"], got["first_high"]]).astype(BF)
        return order(jnp.concatenate([lower, upper], axis=0))


def inverse_rms(x):
    return lax.rsqrt(jnp.mean(x * x, axis=1, keepdims=True) + EPSILON)


def norm_back(grad, x, inv, gain):
    inner = jnp.sum(grad * gain * x, axis=1, keepdims=True)
    back = inv * gain * grad - x * inv**3 * inner / x.shape[1]
    return back, jnp.sum(grad * x * inv, axis=0)


def key_weights(queries, keys, cameras, texts, padded, tail):
    scores = mm_nt(queries, keys) * HD ** (-0.5)
    place = lax.broadcasted_iota(jnp.int32, scores.shape, 1)
    text = CAMS * IMG
    seen = (place < cameras * IMG) | ((place >= text) & (place < text + texts))
    if keys.shape[0] > padded:
        seen = seen | ((place >= padded) & (place < padded + tail))
    scores = jnp.where(seen, scores, MASKED)
    terms = jnp.exp(scores - jnp.max(scores, axis=1, keepdims=True))
    return terms / jnp.sum(terms, axis=1, keepdims=True)


def attend_kernel(padded, tail, cams_ref, texts_ref, q_ref, k_ref, v_ref, mixed_ref):
    weights = key_weights(q_ref[...], k_ref[...], cams_ref[0], texts_ref[0], padded, tail)
    mixed_ref[...] = mm(weights.astype(BF), v_ref[...]).astype(BF)


def attend(cameras, texts, queries, kv, heads, padded, tail, tiles):
    rows, keys = queries.shape[0], kv.shape[0]
    tile = rows // tiles
    return pl.pallas_call(
        functools.partial(attend_kernel, padded, tail),
        grid=(heads, tiles),
        in_specs=[
            pl.BlockSpec(memory_space=pltpu.SMEM),
            pl.BlockSpec(memory_space=pltpu.SMEM),
            pl.BlockSpec((tile, HD), lambda h, i: (i, h)),
            pl.BlockSpec((keys, HD), lambda h, i: (0, 0)),
            pl.BlockSpec((keys, HD), lambda h, i: (0, 1)),
        ],
        out_specs=pl.BlockSpec((tile, HD), lambda h, i: (i, h)),
        out_shape=jax.ShapeDtypeStruct((rows, heads * HD), BF),
        compiler_params=pltpu.CompilerParams(vmem_limit_bytes=VMEM),
        cost_estimate=BRIEF,
        name="attend",
    )(cameras, texts, queries, kv, kv)


def attend_back_kernel(
    padded, tail, cams_ref, texts_ref, q_ref, gm_ref, k_ref, v_ref, start_ref, gq_ref, gkv_ref, sum_ref
):
    first = (pl.program_id(0) == 0) & (pl.program_id(1) == 0)
    last = (pl.program_id(0) == pl.num_programs(0) - 1) & (
        pl.program_id(1) == pl.num_programs(1) - 1
    )
    keys = k_ref.shape[0]

    @pl.when(first)
    def _():
        sum_ref[...] = start_ref[...]

    queries, grad_mixed = q_ref[...], gm_ref[...]
    weights = key_weights(queries, k_ref[...], cams_ref[0], texts_ref[0], padded, tail)
    grad = mm_nt(grad_mixed, v_ref[...])
    inner = jnp.sum(weights * grad, axis=1, keepdims=True)
    grad = (weights * (grad - inner)).astype(BF)
    gq_ref[...] = (mm(grad, k_ref[...]) * HD ** (-0.5)).astype(BF)
    sum_ref[:keys, :HD] += mm_tn(grad, queries) * HD ** (-0.5)
    sum_ref[:keys, HD:] += mm_tn(weights.astype(BF), grad_mixed)

    @pl.when(last)
    def _():
        gkv_ref[...] = sum_ref[...].astype(gkv_ref.dtype)


def attend_back(cameras, texts, queries, grad_mixed, kv, start, kind, heads, padded, tail, tiles, keys):
    rows = queries.shape[0]
    tile = rows // tiles
    return pl.pallas_call(
        functools.partial(attend_back_kernel, padded, tail),
        grid=(heads, tiles),
        in_specs=[
            pl.BlockSpec(memory_space=pltpu.SMEM),
            pl.BlockSpec(memory_space=pltpu.SMEM),
            pl.BlockSpec((tile, HD), lambda h, i: (i, h)),
            pl.BlockSpec((tile, HD), lambda h, i: (i, h)),
            pl.BlockSpec((keys, HD), lambda h, i: (0, 0)),
            pl.BlockSpec((keys, HD), lambda h, i: (0, 1)),
            pl.BlockSpec(start.shape, lambda h, i: (0, 0)),
        ],
        out_specs=[
            pl.BlockSpec((tile, HD), lambda h, i: (i, h)),
            pl.BlockSpec(start.shape, lambda h, i: (0, 0)),
        ],
        out_shape=[
            jax.ShapeDtypeStruct((rows, heads * HD), BF),
            jax.ShapeDtypeStruct(start.shape, kind),
        ],
        scratch_shapes=[pltpu.VMEM(start.shape, F32)],
        compiler_params=pltpu.CompilerParams(vmem_limit_bytes=VMEM),
        cost_estimate=BRIEF,
        name="attend_back",
    )(cameras, texts, queries, grad_mixed, kv, kv, start)


def pair_grad_kernel(pre_ref, by_pre_ref, act_ref, by_act_ref, out_ref):
    depth = pre_ref.shape[1]
    out_ref[0, :depth] = mm_tn(pre_ref[...], by_pre_ref[...]).astype(BF)
    act = act_ref[...] if len(act_ref.shape) == 2 else act_ref[0]
    out_ref[0, depth:] = mm_tn(act, by_act_ref[...]).astype(BF)


def pair_grad(pre, by_pre, act, by_act, n):
    depth, adepth, cols = pre.shape[1] // n, act.shape[1] // n, by_pre.shape[1]
    act_spec = pl.BlockSpec((act.shape[0], adepth), lambda i: (0, i))
    if adepth % 128:
        act = act.reshape(-1, n, adepth).transpose(1, 0, 2)
        act_spec = pl.BlockSpec((1,) + act.shape[1:], lambda i: (i, 0, 0))
    return pl.pallas_call(
        pair_grad_kernel,
        grid=(n,),
        in_specs=[
            pl.BlockSpec((pre.shape[0], depth), lambda i: (0, i)),
            pl.BlockSpec(by_pre.shape, lambda i: (0, 0)),
            act_spec,
            pl.BlockSpec(by_act.shape, lambda i: (0, 0)),
        ],
        out_specs=pl.BlockSpec((1, depth + adepth, cols), lambda i: (i, 0, 0)),
        out_shape=jax.ShapeDtypeStruct((n, depth + adepth, cols), BF),
        compiler_params=pltpu.CompilerParams(vmem_limit_bytes=VMEM),
        cost_estimate=BRIEF,
        name="pair_grad",
    )(pre, by_pre, act, by_act)


def cuts_of(sizes):
    at = 0
    for size in sizes:
        yield slice(at, at + size)
        at += size


def pack_kernel(sizes, gate_ref, up_ref, down_ref, *outs):
    for units, cut, out in zip(sizes, cuts_of(sizes), outs):
        out[0, :, :units] = gate_ref[:, cut]
        out[0, :, units : 2 * units] = up_ref[:, cut]
        out[0, :, 2 * units :] = down_ref[cut, :].astype(F32).T.astype(BF)


def unit_blocks(gate, up, down, n, sizes):
    depth, block = gate.shape[0], gate.shape[1] // n
    if block % 128:
        return [
            jnp.concatenate(
                [
                    gate.reshape(depth, n, block).transpose(1, 0, 2),
                    up.reshape(depth, n, block).transpose(1, 0, 2),
                    down.reshape(n, block, depth).transpose(0, 2, 1),
                ],
                axis=2,
            )
        ]
    return pl.pallas_call(
        functools.partial(pack_kernel, sizes),
        grid=(n,),
        in_specs=[
            pl.BlockSpec((depth, block), lambda i: (0, i)),
            pl.BlockSpec((depth, block), lambda i: (0, i)),
            pl.BlockSpec((block, depth), lambda i: (i, 0)),
        ],
        out_specs=[pl.BlockSpec((1, depth, 3 * units), lambda i: (i, 0, 0)) for units in sizes],
        out_shape=[jax.ShapeDtypeStruct((n, depth, 3 * units), BF) for units in sizes],
        compiler_params=pltpu.CompilerParams(vmem_limit_bytes=VMEM),
        cost_estimate=BRIEF,
        name="pack",
    )(gate, up, down)


def beside(blocks, units):
    n, rows, cols = blocks.shape
    groups = 3 * units // cols
    each = -(-rows // (16 * groups)) * 16
    blocks = jnp.pad(blocks, ((0, 0), (0, each * groups - rows), (0, 0)))
    return jnp.concatenate(jnp.split(blocks, groups, axis=1), axis=2)


def apart(blocks, units, rows):
    groups = blocks.shape[2] // (3 * units)
    return jnp.concatenate(jnp.split(blocks, groups, axis=2), axis=1)[:, :rows]


def unpack_kernel(*refs):
    parts, (gate_ref, up_ref, down_ref) = refs[:-3], refs[-3:]
    sizes = [part.shape[2] // 3 for part in parts]
    for units, cut, part in zip(sizes, cuts_of(sizes), parts):
        gate_ref[:, cut] = part[0, :, :units].astype(F32)
        up_ref[:, cut] = part[0, :, units : 2 * units].astype(F32)
        down_ref[cut, :] = part[0, :, 2 * units :].astype(F32).T


def unblock(parts, depth=None):
    n = parts[0].shape[0]
    depth = depth or parts[0].shape[1]
    block = sum(part.shape[2] // 3 for part in parts)
    if block % 128:
        part = parts[0][:, :depth]
        gate = part[:, :, :block].transpose(1, 0, 2).reshape(depth, n * block)
        up = part[:, :, block : 2 * block].transpose(1, 0, 2).reshape(depth, n * block)
        down = part[:, :, 2 * block :].transpose(0, 2, 1).reshape(n * block, depth)
        return gate.astype(F32), up.astype(F32), down.astype(F32)
    return pl.pallas_call(
        unpack_kernel,
        grid=(n,),
        in_specs=[
            pl.BlockSpec((1, depth, part.shape[2]), lambda i: (i, 0, 0)) for part in parts
        ],
        out_specs=[
            pl.BlockSpec((depth, block), lambda i: (0, i)),
            pl.BlockSpec((depth, block), lambda i: (0, i)),
            pl.BlockSpec((block, depth), lambda i: (i, 0)),
        ],
        out_shape=[
            jax.ShapeDtypeStruct((depth, n * block), F32),
            jax.ShapeDtypeStruct((depth, n * block), F32),
            jax.ShapeDtypeStruct((n * block, depth), F32),
        ],
        compiler_params=pltpu.CompilerParams(vmem_limit_bytes=VMEM),
        cost_estimate=BRIEF,
        name="unpack",
    )(*parts)


class Order:
    def __init__(self):
        self.token = jnp.zeros((8, 128), F32)

    def __call__(self, *values):
        *values, self.token = lax.optimization_barrier(values + (self.token,))
        return values[0] if len(values) == 1 else tuple(values)


def solution(mesh):
    n, k = mesh.shape["dp"], mesh.shape["mp"]

    def per_device(
        prefix_tokens,
        action_tokens,
        camera_counts,
        text_lengths,
        prefix_attn_gain,
        prefix_query_proj,
        prefix_kv_proj,
        prefix_out_proj,
        prefix_ffn_gain,
        prefix_gate_proj,
        prefix_up_proj,
        prefix_down_proj,
        action_attn_gain,
        action_query_proj,
        action_kv_proj,
        action_out_proj,
        action_ffn_gain,
        action_gate_proj,
        action_up_proj,
        action_down_proj,
        prefix_cotangent,
        action_cotangent,
    ):
        mine, me = lax.axis_index("mp"), lax.axis_index("dp")
        rows, wide = prefix_tokens.shape
        arows, awide = action_tokens.shape
        block = -(-rows // (16 * k)) * 16
        padded = block * k
        apad = -(-arows // 64) * 64
        width, awidth = wide * k, awide * k
        fold = apad * awidth // width
        heads = prefix_query_proj.shape[1] // HD
        qcols = heads * HD
        kvcols = prefix_kv_proj.shape[1]
        depth, adepth = prefix_query_proj.shape[0], action_query_proj.shape[0]
        units = prefix_gate_proj.shape[1] // n
        sizes = [units // 2] * 2 if units % 256 == 0 else [units]
        pieces = len(sizes)

        order = Order()

        with jax.named_scope("token_features"):
            x_act = pad_rows(action_tokens, apad)
            x_all = jnp.concatenate(
                [pad_rows(prefix_tokens, padded), x_act.reshape(-1, wide)], axis=0
            )
            x_all = everyones(order(x_all), k)
            gains = jnp.concatenate(
                [prefix_attn_gain, prefix_ffn_gain, action_attn_gain, action_ffn_gain]
            )[None]
            gains = everyones(gains, k)

        with jax.named_scope("cotangents"):
            g_act = everyones(pad_rows(action_cotangent, apad), k)
            g_pre = handed(pad_rows(prefix_cotangent, padded), mine, k, 0)

        with jax.named_scope("attention_weights"):
            qkv_pre = jnp.concatenate([prefix_query_proj, prefix_kv_proj], axis=1)
            wqkv_pre = lax.all_gather(order(qkv_pre), "dp", axis=0, tiled=True)
            group = qcols // kvcols
            wout_pre = lax.all_gather(order(prefix_out_proj.T), "dp", axis=0, tiled=True)
            rest = jnp.concatenate(
                [action_out_proj.T, action_query_proj]
                + [jnp.concatenate(jnp.split(action_kv_proj, group, axis=0), axis=1)],
                axis=0,
            )

        with jax.named_scope("unit_weights"):
            packed = list(
                unit_blocks(prefix_gate_proj, prefix_up_proj, prefix_down_proj, n, sizes)
            )
            own = [exchange(order(packed[0])).reshape(width, 3 * sizes[0])]

        with jax.named_scope("token_features"):
            g_pre = placed(order(*g_pre), mine, 1)
            g_act = placed(order(*g_act), mine, 1)
            g_rows = order(jnp.concatenate([g_pre, g_act.reshape(fold, width)], axis=0))
            gall = lax.all_gather(g_rows, "dp", axis=0)
            gains = placed(order(*gains), mine, 0)
            gain_pre = gains[:, :wide].reshape(1, width)
            gain2_pre = gains[:, wide : 2 * wide].reshape(1, width)
            gain_act = gains[:, 2 * wide : 2 * wide + awide].reshape(1, awidth)
            gain2_act = gains[:, 2 * wide + awide :].reshape(1, awidth)
            x_all = order(*x_all)
            x_pre = order(placed([x[:padded] for x in x_all], mine, 1)).astype(F32)
            x_act = placed([x[padded:].reshape(apad, awide) for x in x_all], mine, 1).astype(F32)

        with jax.named_scope("attention"):
            inv_pre = inverse_rms(x_pre)
            normed_pre = order((x_pre * inv_pre * gain_pre).astype(BF))
            qkv_p = order(mm(normed_pre, order(wqkv_pre)).astype(BF))
            kv_p = everyones(qkv_p[:, qcols:], k)
            kv_p = placed(order(*kv_p), mine, 1)
            tiles = k
            mixed_pre = order(
                attend(camera_counts, text_lengths, qkv_p, kv_p, heads, padded, 0, tiles)
            )
            own[0] = order(own[0])
            branch_pre = order(mm_nt(mixed_pre, order(wout_pre)).astype(BF))
            branch_pre = handed(branch_pre, mine, k, 0)

            xrow_pre = lax.dynamic_slice_in_dim(x_pre, mine * block, block, 0)
            middle_pre = xrow_pre + total(order(*branch_pre))
            inv2_pre = inverse_rms(middle_pre)
            normed2_pre = order((middle_pre * inv2_pre * gain2_pre).astype(BF))
            nall = lax.all_gather(normed2_pre, "dp", axis=0)

            spread = [Spread(order(own[0]), k)]
            aunits = action_gate_proj.shape[1] // n
            [w_act] = unit_blocks(action_gate_proj, action_up_proj, action_down_proj, n, [aunits])
            w_act = exchange(order(w_act))
            rest = lax.all_gather(order(rest), "dp", axis=0)
            spread[0].arrive(order)

        with jax.named_scope("geglu"):
            w_act = order(w_act).reshape(awidth, 3 * aunits)
            gu_act, dt_act = w_act[:, : 2 * aunits], w_act[:, 2 * aunits :]
            gall, nall = order(gall, nall)
            if pieces == 2:
                own.append(exchange(order(packed[1])).reshape(width, 3 * sizes[1]))
            hiddens = [[None] * k for _ in range(pieces)]
            grads = [[None] * k for _ in range(pieces)]
            collects = [Collect(k) for _ in range(pieces)]
            outward = list(range(k - 1, -1, -1))

            def forward(c, s):
                hidden, grad = geglu(order(nall), gall, spread[c].blocks[s], block)
                hiddens[c][s], grads[c][s] = order(hidden, grad)

            def backward(c, s):
                part = weight_grad(order(nall), gall, grads[c][s], hiddens[c][s], block)
                return order(part)

            for s in range(k if k != 4 else 3):
                forward(0, s)
            spread[0].last(order)
            if k == 4:
                forward(0, 3)

            rest = order(rest)
            wout_act = rest[:, :adepth].reshape(n * adepth, qcols)
            wq_act = rest[:, adepth : 2 * adepth].reshape(n * adepth, qcols)
            wkv_act = jnp.concatenate(
                jnp.split(rest[:, 2 * adepth :], group, axis=2), axis=1
            ).reshape(n * adepth, kvcols)
            inv_act = inverse_rms(x_act)
            normed_act = (x_act * inv_act * gain_act).astype(BF)
            q_act, kv_a = order(mm(normed_act, wq_act).astype(BF), mm(normed_act, wkv_act).astype(BF))
            kv_a = everyones(kv_a, k)
            parts = [None] * k
            parts[1] = backward(0, 1)
            kv_a = placed(order(*kv_a), mine, 1)
            kv_all = order(jnp.concatenate([kv_p, kv_a], axis=0))
            mixed_act = order(
                attend(camera_counts, text_lengths, q_act, kv_all, heads, padded, arows, 1)
            )
            branch_act = everyones(order(mm_nt(mixed_act, wout_act).astype(BF)), k)
            parts[2] = backward(0, 2)
            middle_act = x_act + total(order(*branch_act))
            inv2_act = inverse_rms(middle_act)
            normed2_act = order((middle_act * inv2_act * gain2_act).astype(BF))
            nall_act = lax.all_gather(normed2_act, "dp", axis=0, tiled=True)
            if pieces == 2:
                own[1] = order(own[1])
                spread.append(Spread(own[1], k))
            parts[0] = backward(0, 0)
            if pieces == 2:
                forward(1, 0)

            gall_act = gall[:, block:].reshape(n * apad, awidth)
            both = mm(order(nall_act), gu_act)
            hidden, grad_gate, grad_up = gelu_parts(
                both[:, :aunits], both[:, aunits:], mm(gall_act, dt_act)
            )
            hidden = hidden.astype(BF)
            grad = jnp.concatenate([grad_gate, grad_up], axis=1).astype(BF)
            part = jnp.concatenate([mm_nt(hidden, dt_act), mm_nt(grad, gu_act)], axis=1).astype(BF)
            part = order(part)

            tile = n * block // 4
            gn2 = ffn = None
            if pieces == 2:
                gn2 = order(
                    contract([order(grads[0][0])] + grads[0][1:], spread[0].blocks, 0, tile, 1024, None, F32)
                )
                spread[1].arrive(order)
            halving = Halving(part.reshape(n, apad, 2 * awidth), n, me)
            for s in range(3, k):
                parts[s] = backward(0, s)
            for s in outward:
                collects[0].put(s, parts[s])
            halving.take(order)
            if pieces == 2:
                for s in range(1, k if k != 4 else 3):
                    forward(1, s)
                halving.take(order)
                spread[1].last(order)
                if k == 4:
                    forward(1, 3)
            halving.take(order)
            collects[0].far(order)
            part = halving.result(order)
            out_act = handed(part[:, :awidth], mine, k, 1)
            gn2_act = everyones(part[:, awidth:], k)
            last = pieces - 1
            gn2 = order(
                contract([order(grads[last][0])] + grads[last][1:], spread[last].blocks, 0, tile, 1024, gn2)
            )
            gn2 = lax.psum_scatter(gn2, "dp", scatter_dimension=0, tiled=True)
            collects[0].near(order)
            collects[0].receive(order, "first_low", "second_high")
            gn2_act, out_act = order(*gn2_act), order(*out_act)
            flat = [weights for piece in spread for weights in piece.blocks]
            flat_hiddens = [hidden for piece in hiddens for hidden in piece]
            ffn = order(contract([order(flat_hiddens[0])] + flat_hiddens[1:], flat, 2, tile, 1024))
            ffn = lax.psum_scatter(ffn, "dp", scatter_dimension=0, tiled=True)
            parts = {}
            if pieces == 2:
                parts = {s: backward(1, s) for s in outward}
            back = [collects[0].result(order).reshape(n, depth, 3 * sizes[0])]
            gw_act = jnp.concatenate([mm_tn(nall_act, grad), mm_tn(gall_act, hidden)], axis=1)
            gw_act = gw_act.astype(BF).reshape(n, adepth, 3 * aunits)
            back[0] = exchange(order(jnp.concatenate([back[0], beside(gw_act, sizes[0])], axis=1)))

        with jax.named_scope("middle_norm"):
            back2_pre, gg2_pre = norm_back(order(gn2).astype(F32), middle_pre, inv2_pre, gain2_pre)
            resid_pre = g_pre.astype(F32) + back2_pre
            gb_pre = everyones(order(resid_pre.astype(BF)), k)
            for s in parts:
                collects[1].put(s, order(parts[s]))

            gn2_act, out_act = total(gn2_act), total(out_act)
            output_act = (
                lax.dynamic_slice_in_dim(middle_act, mine * awide, awide, 1) + out_act
            )[:arows]
            back2_act, gg2_act = norm_back(order(gn2_act), middle_act, inv2_act, gain2_act)
            resid_act = g_act.astype(F32) + back2_act
            gb_act = resid_act.astype(BF)
            gm_act = order(mm(gb_act, wout_act).astype(BF))
            start = jnp.zeros((padded + apad, 2 * HD), F32)
            gq_act, start = order(
                *attend_back(
                    camera_counts, text_lengths, q_act, gm_act, kv_all, start, F32,
                    heads, padded, arows, 1, padded + apad,
                )
            )
            gb_pre = placed(order(*gb_pre), mine, 0)
            back[0] = order(back[0])
            if pieces == 2:
                collects[1].far(order)
                collects[1].near(order)

        with jax.named_scope("attention_back"):
            gm_pre = order(mm(gb_pre, wout_pre).astype(BF))
            gq_pre, gkv = order(
                *attend_back(
                    camera_counts, text_lengths, qkv_p, gm_pre, kv_p, start, BF,
                    heads, padded, 0, tiles, padded,
                )
            )
            gkv = handed(gkv, mine, k, 1)
            go = order(pair_grad(gb_pre, mixed_pre, gb_act, mixed_act, n)).reshape(-1, qcols)
            go = lax.psum_scatter(go, "dp", scatter_dimension=0, tiled=True)
            gkv = total(order(*gkv)).astype(BF)
            gqkv_pre = order(jnp.concatenate([gq_pre, gkv[:padded]], axis=1))
            gqkv_act = jnp.concatenate([gq_act, gkv[padded:]], axis=1)
            gn_pre = order(mm_nt(gqkv_pre, wqkv_pre).astype(BF))
            gn_pre = handed(gn_pre, mine, k, 0)
            gn_act = (mm_nt(gq_act, wq_act) + mm_nt(gkv[padded:], wkv_act)).astype(BF)
            gn_act = everyones(order(gn_act), k)

        with jax.named_scope("query_key_value_grads"):
            gw = order(pair_grad(order(normed_pre), gqkv_pre, normed_act, gqkv_act, n))
            gw = gw.reshape(-1, qcols + kvcols)
            gw = lax.psum_scatter(gw, "dp", scatter_dimension=0, tiled=True)
            if pieces == 2:
                back1 = collects[1].result(order).reshape(n, depth, 3 * sizes[1])
                back.append(exchange(order(back1)))

        with jax.named_scope("input_grads"):
            gn_pre = total(order(*gn_pre))
            invrow = lax.dynamic_slice_in_dim(inv_pre, mine * block, block, 0)
            back_pre, gg_pre = norm_back(gn_pre, xrow_pre, invrow, gain_pre)
            in_pre = order((resid_pre + back_pre).astype(BF))
            in_pre = handed(in_pre, mine, k, 1)
            out_pre = order((middle_pre + order(ffn).astype(F32)).astype(BF))
            out_pre = handed(out_pre, mine, k, 1)
            gn_act = total(order(*gn_act))
            back_act, gg_act = norm_back(gn_act, x_act, inv_act, gain_act)
            in_act = lax.dynamic_slice_in_dim(resid_act + back_act, mine * awide, awide, 1)[:arows]

        with jax.named_scope("gain_grads"):

            def gain_sum(pre, act):
                pre = sum(handed(jnp.stack(pre), mine, k, 1))
                act = lax.dynamic_slice_in_dim(jnp.stack(act), mine * awide, awide, 1)
                both = butterfly_sum(order(jnp.concatenate([pre, act], axis=1)), n)
                return both[0, :wide], both[1, :wide], both[0, wide:], both[1, wide:]

            gg_pre, gg2_pre, gg_act, gg2_act = gain_sum((gg_pre, gg2_pre), (gg_act, gg2_act))

        with jax.named_scope("unit_weight_grads"):
            gw_act = apart(back[0][:, depth:], aunits, adepth)
            gate_act, up_act, down_act = unblock([gw_act])
            in_pre = placed(order(*in_pre), mine, 0)[:rows].astype(F32)
            output_pre = placed(order(*out_pre), mine, 0)[:rows].astype(F32)
            go = order(go).astype(F32)
            gw = order(gw).astype(F32)
            if pieces == 2:
                back[1] = order(back[1])
            gate_pre, up_pre, down_pre = unblock(back, depth)
            gg_pre = gg_pre + order.token[0, 0]
        return (
            output_pre,
            output_act,
            in_pre,
            in_act,
            gg_pre,
            gw[:depth, :qcols],
            gw[:depth, qcols:],
            go[:depth].T,
            gg2_pre,
            gate_pre,
            up_pre,
            down_pre,
            gg_act,
            gw[depth:, :qcols],
            gw[depth:, qcols:],
            go[depth:].T,
            gg2_act,
            gate_act,
            up_act,
            down_act,
        )

    split, rowsplit, whole = P("dp", "mp"), P("mp", "dp"), P("mp")
    weights = (whole, split, split, rowsplit, whole, split, split, rowsplit)
    return jax.shard_map(
        per_device,
        mesh=mesh,
        in_specs=(split, split, P("dp"), P("dp")) + weights + weights + (split, split),
        out_specs=(split, split, split, split) + weights + weights,
        check_vma=False,
    )
```

```python
import functools

import jax
import jax.numpy as jnp
from jax import lax
from jax.experimental import pallas as pl
from jax.experimental.pallas import tpu as pltpu
from jax.sharding import PartitionSpec as P

HD = 256
IMG = 256
CAMS = 3
EPSILON = 1e-06
MASKED = -1e30
BF = jnp.bfloat16
F32 = jnp.float32
SLOPE = 0.7978845608028654
CUBE = 0.044715
VMEM = 56 * 2**20
BRIEF = pl.CostEstimate(flops=1, bytes_accessed=1, transcendentals=0)


def dot(a, b, over_a, over_b):
    return lax.dot_general(a, b, (((over_a,), (over_b,)), ((), ())), preferred_element_type=F32)


def mm(a, b):
    return dot(a, b, 1, 0)


def mm_tn(a, b):
    return dot(a, b, 0, 0)


def mm_nt(a, b):
    return dot(a, b, 1, 1)


def gelu_parts(gate, up, grad_hidden):
    square = gate * gate
    tanh = jnp.tanh(SLOPE * gate * (1.0 + CUBE * square))
    half = 0.5 * (1.0 + tanh)
    act = gate * half
    slope = half + 0.5 * gate * (1.0 - tanh * tanh) * (SLOPE * (1.0 + 3.0 * CUBE * square))
    return act * up, grad_hidden * up * slope, grad_hidden * act


def geglu_kernel(n_ref, g_ref, gate_up_ref, down_ref, hidden_ref, grad_ref):
    units = down_ref.shape[1]
    rows = n_ref.shape[0] * n_ref.shape[1]
    width = n_ref.shape[2]
    both = mm(n_ref[...].reshape(rows, width), gate_up_ref[...])
    grad_hidden = mm(g_ref[...].reshape(rows, width), down_ref[...])
    hidden, grad_gate, grad_up = gelu_parts(both[:, :units], both[:, units:], grad_hidden)
    hidden_ref[...] = hidden.astype(BF)
    grad_ref[:, :units] = grad_gate.astype(BF)
    grad_ref[:, units:] = grad_up.astype(BF)


def geglu(normed, cots, weights, block, step=2):
    n, _, width = normed.shape
    units = weights.shape[1] // 3
    rows = step * block
    return pl.pallas_call(
        geglu_kernel,
        grid=(n // step,),
        in_specs=[
            pl.BlockSpec((step, block, width), lambda i: (i, 0, 0)),
            pl.BlockSpec((step, block, width), lambda i: (i, 0, 0)),
            pl.BlockSpec((width, 2 * units), lambda i: (0, 0)),
            pl.BlockSpec((width, units), lambda i: (0, 2)),
        ],
        out_specs=[
            pl.BlockSpec((rows, units), lambda i: (i, 0)),
            pl.BlockSpec((rows, 2 * units), lambda i: (i, 0)),
        ],
        out_shape=[
            jax.ShapeDtypeStruct((n * block, units), BF),
            jax.ShapeDtypeStruct((n * block, 2 * units), BF),
        ],
        compiler_params=pltpu.CompilerParams(vmem_limit_bytes=VMEM),
        cost_estimate=BRIEF,
        name="geglu",
    )(normed, cots, weights, weights)


def contract_kernel(count, *refs):
    out = refs[-1]
    total = mm_nt(refs[0][...], refs[count][...])
    for s in range(1, count):
        total += mm_nt(refs[s][...], refs[count + s][...])
    if len(refs) > 2 * count + 1:
        total += refs[2 * count][...]
    out[...] = total.astype(out.dtype)


def contract(parts, weights, column, tile, cols, base=None, kind=BF):
    count, rows = len(parts), parts[0].shape[0]
    width = weights[0].shape[0]
    bases = [] if base is None else [base]
    return pl.pallas_call(
        functools.partial(contract_kernel, count),
        grid=(width // cols, rows // tile),
        in_specs=[pl.BlockSpec((tile, part.shape[1]), lambda j, i: (i, 0)) for part in parts]
        + [pl.BlockSpec((cols, part.shape[1]), lambda j, i: (j, column)) for part in parts]
        + [pl.BlockSpec((tile, cols), lambda j, i: (i, j))] * len(bases),
        out_specs=pl.BlockSpec((tile, cols), lambda j, i: (i, j)),
        out_shape=jax.ShapeDtypeStruct((rows, width), kind),
        compiler_params=pltpu.CompilerParams(vmem_limit_bytes=VMEM),
        cost_estimate=BRIEF,
        name="contract",
    )(*parts, *weights, *bases)


def weight_grad_kernel(n_ref, g_ref, grad_ref, hidden_ref, out_ref):
    rows, cols = n_ref.shape[0] * n_ref.shape[1], n_ref.shape[2]
    units = hidden_ref.shape[1]
    out_ref[:, : 2 * units] = mm_tn(n_ref[...].reshape(rows, cols), grad_ref[...]).astype(BF)
    out_ref[:, 2 * units :] = mm_tn(g_ref[...].reshape(rows, cols), hidden_ref[...]).astype(BF)


def weight_grad(normed, cots, grad, hidden, block, cols=512):
    n, _, width = normed.shape
    units = hidden.shape[1]
    rows = n * block
    return pl.pallas_call(
        weight_grad_kernel,
        grid=(width // cols,),
        in_specs=[
            pl.BlockSpec((n, block, cols), lambda i: (0, 0, i)),
            pl.BlockSpec((n, block, cols), lambda i: (0, 0, i)),
            pl.BlockSpec((rows, 2 * units), lambda i: (0, 0)),
            pl.BlockSpec((rows, units), lambda i: (0, 0)),
        ],
        out_specs=pl.BlockSpec((cols, 3 * units), lambda i: (i, 0)),
        out_shape=jax.ShapeDtypeStruct((width, 3 * units), BF),
        compiler_params=pltpu.CompilerParams(vmem_limit_bytes=VMEM),
        cost_estimate=BRIEF,
        name="weight_grad",
    )(normed, cots, grad, hidden)


def pad_rows(a, rows):
    return jnp.pad(a, ((0, rows - a.shape[0]), (0, 0)))


def swap(a, axis, size, step):
    return lax.ppermute(a, axis, [(i, i ^ step) for i in range(size)])


def exchange(a):
    return lax.all_to_all(a, "dp", 0, 0, tiled=True)


def everyones(a, k):
    return [a] + [swap(a, "mp", k, s) for s in range(1, k)]


def placed(parts, mine, axis):
    size = parts[0].shape[axis]
    shape = list(parts[0].shape)
    shape[axis] *= len(parts)
    whole = jnp.zeros(shape, parts[0].dtype)
    for s, part in enumerate(parts):
        whole = lax.dynamic_update_slice_in_dim(whole, part, (mine ^ s) * size, axis)
    return whole


def handed(a, mine, k, axis):
    size = a.shape[axis] // k
    cut = [lax.dynamic_slice_in_dim(a, (mine ^ s) * size, size, axis) for s in range(k)]
    return [cut[0]] + [swap(cut[s], "mp", k, s) for s in range(1, k)]


def total(parts):
    return sum(part.astype(F32) for part in parts)


def butterfly_sum(a, n):
    step = 1
    while step < n:
        a = a + swap(a, "dp", n, step)
        step *= 2
    return a


class Halving:
    def __init__(self, a, n, me):
        self.a, self.n, self.me, self.step = a, n, me, 1
        self.send()

    def send(self):
        if self.step == self.n:
            return
        a = self.a
        pairs = a.reshape((a.shape[0] // 2, 2) + a.shape[1:])
        bit = (self.me // self.step) % 2
        self.keep = lax.dynamic_index_in_dim(pairs, bit, 1, keepdims=False)
        send = lax.dynamic_index_in_dim(pairs, 1 - bit, 1, keepdims=False)
        self.got = swap(send, "dp", self.n, self.step)

    def take(self, order):
        if self.step == self.n:
            return
        self.a = (self.keep.astype(F32) + order(self.got).astype(F32)).astype(BF)
        self.step *= 2
        self.send()

    def result(self, order):
        while self.step < self.n:
            self.take(order)
        return self.a[0]


class Spread:
    def __init__(self, block, k):
        self.k = k
        if k == 4:
            self.blocks = [block, swap(block, "mp", k, 1), swap(block, "mp", k, 2)]
        else:
            self.blocks = everyones(block, k)

    def arrive(self, order):
        self.blocks[1:] = order(*self.blocks[1:])
        if self.k == 4:
            half = self.blocks[0].shape[0] // 2
            self.low = swap(self.blocks[2][:half], "mp", 4, 1)
            self.high = swap(self.blocks[1][half:], "mp", 4, 2)

    def last(self, order):
        if self.k == 4:
            self.blocks.append(order(jnp.concatenate(order(self.low, self.high), axis=0)))


class Collect:
    def __init__(self, k):
        self.k, self.parts, self.got = k, {}, {}

    def put(self, s, part):
        self.parts[s] = part
        half = part.shape[0] // 2
        if self.k != 4:
            if s:
                self.got[s] = swap(part, "mp", self.k, s)
        elif s == 3:
            self.low = swap(part[:half], "mp", 4, 1)
            self.high = swap(part[half:], "mp", 4, 2)
        elif s == 1:
            self.got["first_low"] = swap(part[:half], "mp", 4, 1)
        elif s == 2:
            self.got["second_high"] = swap(part[half:], "mp", 4, 2)

    def receive(self, order, *names):
        for name in names:
            if name in self.got:
                self.got[name] = order(self.got[name])

    def far(self, order):
        if self.k == 4:
            self.low, self.high = order(self.low, self.high)

    def near(self, order):
        if self.k == 4:
            half = self.low.shape[0]
            low, high = order(
                total([self.parts[2][:half], self.low]).astype(BF),
                total([self.parts[1][half:], self.high]).astype(BF),
            )
            self.got["second_low"] = swap(low, "mp", 4, 2)
            self.got["first_high"] = swap(high, "mp", 4, 1)

    def result(self, order):
        own, got = self.parts[0], self.got
        if self.k != 4:
            return order(total([own, *order(*got.values())]).astype(BF))
        self.receive(order, "first_low", "second_high", "second_low", "first_high")
        half = self.low.shape[0]
        lower = total([own[:half], got["first_low"], got["second_low"]]).astype(BF)
        upper = total([own[half:], got["second_high"], got["first_high"]]).astype(BF)
        return order(jnp.concatenate([lower, upper], axis=0))


def inverse_rms(x):
    return lax.rsqrt(jnp.mean(x * x, axis=1, keepdims=True) + EPSILON)


def norm_back(grad, x, inv, gain):
    inner = jnp.sum(grad * gain * x, axis=1, keepdims=True)
    back = inv * gain * grad - x * inv**3 * inner / x.shape[1]
    return back, jnp.sum(grad * x * inv, axis=0)


def key_weights(queries, keys, cameras, texts, padded, tail):
    scores = mm_nt(queries, keys) * HD ** (-0.5)
    place = lax.broadcasted_iota(jnp.int32, scores.shape, 1)
    text = CAMS * IMG
    seen = (place < cameras * IMG) | ((place >= text) & (place < text + texts))
    if keys.shape[0] > padded:
        seen = seen | ((place >= padded) & (place < padded + tail))
    scores = jnp.where(seen, scores, MASKED)
    terms = jnp.exp(scores - jnp.max(scores, axis=1, keepdims=True))
    return terms / jnp.sum(terms, axis=1, keepdims=True)


def attend_kernel(padded, tail, cams_ref, texts_ref, q_ref, k_ref, v_ref, mixed_ref):
    weights = key_weights(q_ref[...], k_ref[...], cams_ref[0], texts_ref[0], padded, tail)
    mixed_ref[...] = mm(weights.astype(BF), v_ref[...]).astype(BF)


def attend(cameras, texts, queries, kv, heads, padded, tail, tiles):
    rows, keys = queries.shape[0], kv.shape[0]
    tile = rows // tiles
    return pl.pallas_call(
        functools.partial(attend_kernel, padded, tail),
        grid=(heads, tiles),
        in_specs=[
            pl.BlockSpec(memory_space=pltpu.SMEM),
            pl.BlockSpec(memory_space=pltpu.SMEM),
            pl.BlockSpec((tile, HD), lambda h, i: (i, h)),
            pl.BlockSpec((keys, HD), lambda h, i: (0, 0)),
            pl.BlockSpec((keys, HD), lambda h, i: (0, 1)),
        ],
        out_specs=pl.BlockSpec((tile, HD), lambda h, i: (i, h)),
        out_shape=jax.ShapeDtypeStruct((rows, heads * HD), BF),
        compiler_params=pltpu.CompilerParams(vmem_limit_bytes=VMEM),
        cost_estimate=BRIEF,
        name="attend",
    )(cameras, texts, queries, kv, kv)


def attend_back_kernel(
    padded, tail, cams_ref, texts_ref, q_ref, gm_ref, k_ref, v_ref, start_ref, gq_ref, gkv_ref, sum_ref
):
    first = (pl.program_id(0) == 0) & (pl.program_id(1) == 0)
    last = (pl.program_id(0) == pl.num_programs(0) - 1) & (
        pl.program_id(1) == pl.num_programs(1) - 1
    )
    keys = k_ref.shape[0]

    @pl.when(first)
    def _():
        sum_ref[...] = start_ref[...]

    queries, grad_mixed = q_ref[...], gm_ref[...]
    weights = key_weights(queries, k_ref[...], cams_ref[0], texts_ref[0], padded, tail)
    grad = mm_nt(grad_mixed, v_ref[...])
    inner = jnp.sum(weights * grad, axis=1, keepdims=True)
    grad = (weights * (grad - inner)).astype(BF)
    gq_ref[...] = (mm(grad, k_ref[...]) * HD ** (-0.5)).astype(BF)
    sum_ref[:keys, :HD] += mm_tn(grad, queries) * HD ** (-0.5)
    sum_ref[:keys, HD:] += mm_tn(weights.astype(BF), grad_mixed)

    @pl.when(last)
    def _():
        gkv_ref[...] = sum_ref[...].astype(gkv_ref.dtype)


def attend_back(cameras, texts, queries, grad_mixed, kv, start, kind, heads, padded, tail, tiles, keys):
    rows = queries.shape[0]
    tile = rows // tiles
    return pl.pallas_call(
        functools.partial(attend_back_kernel, padded, tail),
        grid=(heads, tiles),
        in_specs=[
            pl.BlockSpec(memory_space=pltpu.SMEM),
            pl.BlockSpec(memory_space=pltpu.SMEM),
            pl.BlockSpec((tile, HD), lambda h, i: (i, h)),
            pl.BlockSpec((tile, HD), lambda h, i: (i, h)),
            pl.BlockSpec((keys, HD), lambda h, i: (0, 0)),
            pl.BlockSpec((keys, HD), lambda h, i: (0, 1)),
            pl.BlockSpec(start.shape, lambda h, i: (0, 0)),
        ],
        out_specs=[
            pl.BlockSpec((tile, HD), lambda h, i: (i, h)),
            pl.BlockSpec(start.shape, lambda h, i: (0, 0)),
        ],
        out_shape=[
            jax.ShapeDtypeStruct((rows, heads * HD), BF),
            jax.ShapeDtypeStruct(start.shape, kind),
        ],
        scratch_shapes=[pltpu.VMEM(start.shape, F32)],
        compiler_params=pltpu.CompilerParams(vmem_limit_bytes=VMEM),
        cost_estimate=BRIEF,
        name="attend_back",
    )(cameras, texts, queries, grad_mixed, kv, kv, start)


def pair_grad_kernel(pre_ref, by_pre_ref, act_ref, by_act_ref, out_ref):
    depth = pre_ref.shape[1]
    out_ref[0, :depth] = mm_tn(pre_ref[...], by_pre_ref[...]).astype(BF)
    act = act_ref[...] if len(act_ref.shape) == 2 else act_ref[0]
    out_ref[0, depth:] = mm_tn(act, by_act_ref[...]).astype(BF)


def pair_grad(pre, by_pre, act, by_act, n):
    depth, adepth, cols = pre.shape[1] // n, act.shape[1] // n, by_pre.shape[1]
    act_spec = pl.BlockSpec((act.shape[0], adepth), lambda i: (0, i))
    if adepth % 128:
        act = act.reshape(-1, n, adepth).transpose(1, 0, 2)
        act_spec = pl.BlockSpec((1,) + act.shape[1:], lambda i: (i, 0, 0))
    return pl.pallas_call(
        pair_grad_kernel,
        grid=(n,),
        in_specs=[
            pl.BlockSpec((pre.shape[0], depth), lambda i: (0, i)),
            pl.BlockSpec(by_pre.shape, lambda i: (0, 0)),
            act_spec,
            pl.BlockSpec(by_act.shape, lambda i: (0, 0)),
        ],
        out_specs=pl.BlockSpec((1, depth + adepth, cols), lambda i: (i, 0, 0)),
        out_shape=jax.ShapeDtypeStruct((n, depth + adepth, cols), BF),
        compiler_params=pltpu.CompilerParams(vmem_limit_bytes=VMEM),
        cost_estimate=BRIEF,
        name="pair_grad",
    )(pre, by_pre, act, by_act)


def cuts_of(sizes):
    at = 0
    for size in sizes:
        yield slice(at, at + size)
        at += size


def pack_kernel(sizes, gate_ref, up_ref, down_ref, *outs):
    for units, cut, out in zip(sizes, cuts_of(sizes), outs):
        out[0, :, :units] = gate_ref[:, cut]
        out[0, :, units : 2 * units] = up_ref[:, cut]
        out[0, :, 2 * units :] = down_ref[cut, :].astype(F32).T.astype(BF)


def unit_blocks(gate, up, down, n, sizes):
    depth, block = gate.shape[0], gate.shape[1] // n
    if block % 128:
        return [
            jnp.concatenate(
                [
                    gate.reshape(depth, n, block).transpose(1, 0, 2),
                    up.reshape(depth, n, block).transpose(1, 0, 2),
                    down.reshape(n, block, depth).transpose(0, 2, 1),
                ],
                axis=2,
            )
        ]
    return pl.pallas_call(
        functools.partial(pack_kernel, sizes),
        grid=(n,),
        in_specs=[
            pl.BlockSpec((depth, block), lambda i: (0, i)),
            pl.BlockSpec((depth, block), lambda i: (0, i)),
            pl.BlockSpec((block, depth), lambda i: (i, 0)),
        ],
        out_specs=[pl.BlockSpec((1, depth, 3 * units), lambda i: (i, 0, 0)) for units in sizes],
        out_shape=[jax.ShapeDtypeStruct((n, depth, 3 * units), BF) for units in sizes],
        compiler_params=pltpu.CompilerParams(vmem_limit_bytes=VMEM),
        cost_estimate=BRIEF,
        name="pack",
    )(gate, up, down)


def beside(blocks, units):
    n, rows, cols = blocks.shape
    groups = 3 * units // cols
    each = -(-rows // (16 * groups)) * 16
    blocks = jnp.pad(blocks, ((0, 0), (0, each * groups - rows), (0, 0)))
    return jnp.concatenate(jnp.split(blocks, groups, axis=1), axis=2)


def apart(blocks, units, rows):
    groups = blocks.shape[2] // (3 * units)
    return jnp.concatenate(jnp.split(blocks, groups, axis=2), axis=1)[:, :rows]


def unpack_kernel(*refs):
    parts, (gate_ref, up_ref, down_ref) = refs[:-3], refs[-3:]
    sizes = [part.shape[2] // 3 for part in parts]
    for units, cut, part in zip(sizes, cuts_of(sizes), parts):
        gate_ref[:, cut] = part[0, :, :units].astype(F32)
        up_ref[:, cut] = part[0, :, units : 2 * units].astype(F32)
        down_ref[cut, :] = part[0, :, 2 * units :].astype(F32).T


def unblock(parts, depth=None):
    n = parts[0].shape[0]
    depth = depth or parts[0].shape[1]
    block = sum(part.shape[2] // 3 for part in parts)
    if block % 128:
        part = parts[0][:, :depth]
        gate = part[:, :, :block].transpose(1, 0, 2).reshape(depth, n * block)
        up = part[:, :, block : 2 * block].transpose(1, 0, 2).reshape(depth, n * block)
        down = part[:, :, 2 * block :].transpose(0, 2, 1).reshape(n * block, depth)
        return gate.astype(F32), up.astype(F32), down.astype(F32)
    return pl.pallas_call(
        unpack_kernel,
        grid=(n,),
        in_specs=[
            pl.BlockSpec((1, depth, part.shape[2]), lambda i: (i, 0, 0)) for part in parts
        ],
        out_specs=[
            pl.BlockSpec((depth, block), lambda i: (0, i)),
            pl.BlockSpec((depth, block), lambda i: (0, i)),
            pl.BlockSpec((block, depth), lambda i: (i, 0)),
        ],
        out_shape=[
            jax.ShapeDtypeStruct((depth, n * block), F32),
            jax.ShapeDtypeStruct((depth, n * block), F32),
            jax.ShapeDtypeStruct((n * block, depth), F32),
        ],
        compiler_params=pltpu.CompilerParams(vmem_limit_bytes=VMEM),
        cost_estimate=BRIEF,
        name="unpack",
    )(*parts)


class Order:
    def __init__(self):
        self.token = jnp.zeros((8, 128), F32)

    def __call__(self, *values):
        *values, self.token = lax.optimization_barrier(values + (self.token,))
        return values[0] if len(values) == 1 else tuple(values)


def solution(mesh):
    n, k = mesh.shape["dp"], mesh.shape["mp"]

    def per_device(
        prefix_tokens,
        action_tokens,
        camera_counts,
        text_lengths,
        prefix_attn_gain,
        prefix_query_proj,
        prefix_kv_proj,
        prefix_out_proj,
        prefix_ffn_gain,
        prefix_gate_proj,
        prefix_up_proj,
        prefix_down_proj,
        action_attn_gain,
        action_query_proj,
        action_kv_proj,
        action_out_proj,
        action_ffn_gain,
        action_gate_proj,
        action_up_proj,
        action_down_proj,
        prefix_cotangent,
        action_cotangent,
    ):
        mine, me = lax.axis_index("mp"), lax.axis_index("dp")
        rows, wide = prefix_tokens.shape
        arows, awide = action_tokens.shape
        block = -(-rows // (16 * k)) * 16
        padded = block * k
        apad = -(-arows // 64) * 64
        width, awidth = wide * k, awide * k
        fold = apad * awidth // width
        heads = prefix_query_proj.shape[1] // HD
        qcols = heads * HD
        kvcols = prefix_kv_proj.shape[1]
        depth, adepth = prefix_query_proj.shape[0], action_query_proj.shape[0]
        units = prefix_gate_proj.shape[1] // n
        sizes = [units // 2] * 2 if units % 256 == 0 else [units]
        pieces = len(sizes)

        order = Order()

        with jax.named_scope("token_features"):
            x_act = pad_rows(action_tokens, apad)
            x_all = jnp.concatenate(
                [pad_rows(prefix_tokens, padded), x_act.reshape(-1, wide)], axis=0
            )
            x_all = everyones(order(x_all), k)
            gains = jnp.concatenate(
                [prefix_attn_gain, prefix_ffn_gain, action_attn_gain, action_ffn_gain]
            )[None]
            gains = everyones(gains, k)

        with jax.named_scope("cotangents"):
            g_act = everyones(pad_rows(action_cotangent, apad), k)
            g_pre = handed(pad_rows(prefix_cotangent, padded), mine, k, 0)

        with jax.named_scope("attention_weights"):
            qkv_pre = jnp.concatenate([prefix_query_proj, prefix_kv_proj], axis=1)
            wqkv_pre = lax.all_gather(order(qkv_pre), "dp", axis=0, tiled=True)
            group = qcols // kvcols
            wout_pre = lax.all_gather(order(prefix_out_proj.T), "dp", axis=0, tiled=True)
            rest = jnp.concatenate(
                [action_out_proj.T, action_query_proj]
                + [jnp.concatenate(jnp.split(action_kv_proj, group, axis=0), axis=1)],
                axis=0,
            )

        with jax.named_scope("unit_weights"):
            packed = list(
                unit_blocks(prefix_gate_proj, prefix_up_proj, prefix_down_proj, n, sizes)
            )
            own = [exchange(order(packed[0])).reshape(width, 3 * sizes[0])]

        with jax.named_scope("token_features"):
            g_pre = placed(order(*g_pre), mine, 1)
            g_act = placed(order(*g_act), mine, 1)
            g_rows = order(jnp.concatenate([g_pre, g_act.reshape(fold, width)], axis=0))
            gall = lax.all_gather(g_rows, "dp", axis=0)
            gains = placed(order(*gains), mine, 0)
            gain_pre = gains[:, :wide].reshape(1, width)
            gain2_pre = gains[:, wide : 2 * wide].reshape(1, width)
            gain_act = gains[:, 2 * wide : 2 * wide + awide].reshape(1, awidth)
            gain2_act = gains[:, 2 * wide + awide :].reshape(1, awidth)
            x_all = order(*x_all)
            x_pre = order(placed([x[:padded] for x in x_all], mine, 1)).astype(F32)
            x_act = placed([x[padded:].reshape(apad, awide) for x in x_all], mine, 1).astype(F32)

        with jax.named_scope("attention"):
            inv_pre = inverse_rms(x_pre)
            normed_pre = order((x_pre * inv_pre * gain_pre).astype(BF))
            qkv_p = order(mm(normed_pre, order(wqkv_pre)).astype(BF))
            kv_p = everyones(qkv_p[:, qcols:], k)
            kv_p = placed(order(*kv_p), mine, 1)
            tiles = k
            mixed_pre = order(
                attend(camera_counts, text_lengths, qkv_p, kv_p, heads, padded, 0, tiles)
            )
            own[0] = order(own[0])
            branch_pre = order(mm_nt(mixed_pre, order(wout_pre)).astype(BF))
            branch_pre = handed(branch_pre, mine, k, 0)

            xrow_pre = lax.dynamic_slice_in_dim(x_pre, mine * block, block, 0)
            middle_pre = xrow_pre + total(order(*branch_pre))
            inv2_pre = inverse_rms(middle_pre)
            normed2_pre = order((middle_pre * inv2_pre * gain2_pre).astype(BF))
            nall = lax.all_gather(normed2_pre, "dp", axis=0)

            spread = [Spread(order(own[0]), k)]
            aunits = action_gate_proj.shape[1] // n
            [w_act] = unit_blocks(action_gate_proj, action_up_proj, action_down_proj, n, [aunits])
            w_act = exchange(order(w_act))
            rest = lax.all_gather(order(rest), "dp", axis=0)
            spread[0].arrive(order)

        with jax.named_scope("geglu"):
            w_act = order(w_act).reshape(awidth, 3 * aunits)
            gu_act, dt_act = w_act[:, : 2 * aunits], w_act[:, 2 * aunits :]
            gall, nall = order(gall, nall)
            if pieces == 2:
                own.append(exchange(order(packed[1])).reshape(width, 3 * sizes[1]))
            hiddens = [[None] * k for _ in range(pieces)]
            grads = [[None] * k for _ in range(pieces)]
            collects = [Collect(k) for _ in range(pieces)]
            outward = list(range(k - 1, -1, -1))

            def forward(c, s):
                hidden, grad = geglu(order(nall), gall, spread[c].blocks[s], block)
                hiddens[c][s], grads[c][s] = order(hidden, grad)

            def backward(c, s):
                part = weight_grad(order(nall), gall, grads[c][s], hiddens[c][s], block)
                return order(part)

            for s in range(k if k != 4 else 3):
                forward(0, s)
            spread[0].last(order)
            if k == 4:
                forward(0, 3)

            rest = order(rest)
            wout_act = rest[:, :adepth].reshape(n * adepth, qcols)
            wq_act = rest[:, adepth : 2 * adepth].reshape(n * adepth, qcols)
            wkv_act = jnp.concatenate(
                jnp.split(rest[:, 2 * adepth :], group, axis=2), axis=1
            ).reshape(n * adepth, kvcols)
            inv_act = inverse_rms(x_act)
            normed_act = (x_act * inv_act * gain_act).astype(BF)
            q_act, kv_a = order(mm(normed_act, wq_act).astype(BF), mm(normed_act, wkv_act).astype(BF))
            kv_a = everyones(kv_a, k)
            parts = [None] * k
            parts[1] = backward(0, 1)
            kv_a = placed(order(*kv_a), mine, 1)
            kv_all = order(jnp.concatenate([kv_p, kv_a], axis=0))
            mixed_act = order(
                attend(camera_counts, text_lengths, q_act, kv_all, heads, padded, arows, 1)
            )
            branch_act = everyones(order(mm_nt(mixed_act, wout_act).astype(BF)), k)
            parts[2] = backward(0, 2)
            middle_act = x_act + total(order(*branch_act))
            inv2_act = inverse_rms(middle_act)
            normed2_act = order((middle_act * inv2_act * gain2_act).astype(BF))
            nall_act = lax.all_gather(normed2_act, "dp", axis=0, tiled=True)
            if pieces == 2:
                own[1] = order(own[1])
                spread.append(Spread(own[1], k))
            parts[0] = backward(0, 0)
            if pieces == 2:
                forward(1, 0)

            gall_act = gall[:, block:].reshape(n * apad, awidth)
            both = mm(order(nall_act), gu_act)
            hidden, grad_gate, grad_up = gelu_parts(
                both[:, :aunits], both[:, aunits:], mm(gall_act, dt_act)
            )
            hidden = hidden.astype(BF)
            grad = jnp.concatenate([grad_gate, grad_up], axis=1).astype(BF)
            part = jnp.concatenate([mm_nt(hidden, dt_act), mm_nt(grad, gu_act)], axis=1).astype(BF)
            part = order(part)

            halving = Halving(part.reshape(n, apad, 2 * awidth), n, me)

            tile = n * block // 4
            gn2 = ffn = None
            if pieces == 2:
                gn2 = order(
                    contract([order(grads[0][0])] + grads[0][1:], spread[0].blocks, 0, tile, 1024, None, F32)
                )
            halving.take(order)
            for s in range(3, k):
                parts[s] = backward(0, s)
            halving.take(order)
            if pieces == 2:
                spread[1].arrive(order)
                forward(1, 1)
            halving.take(order)
            part = halving.result(order)
            out_act = handed(part[:, :awidth], mine, k, 1)
            gn2_act = everyones(part[:, awidth:], k)
            if pieces == 2:
                for s in range(2, k if k != 4 else 3):
                    forward(1, s)
                spread[1].last(order)
                if k == 4:
                    forward(1, 3)
            gn2_act, out_act = order(*gn2_act), order(*out_act)
            for s in outward:
                collects[0].put(s, order(parts[s]))
            last = pieces - 1
            gn2 = order(
                contract([order(grads[last][0])] + grads[last][1:], spread[last].blocks, 0, tile, 1024, gn2)
            )
            gn2 = lax.psum_scatter(gn2, "dp", scatter_dimension=0, tiled=True)
            collects[0].far(order)
            flat = [weights for piece in spread for weights in piece.blocks]
            flat_hiddens = [hidden for piece in hiddens for hidden in piece]
            ffn = order(contract([order(flat_hiddens[0])] + flat_hiddens[1:], flat, 2, tile, 1024))
            ffn = lax.psum_scatter(ffn, "dp", scatter_dimension=0, tiled=True)
            parts = {}
            if pieces == 2:
                parts = {s: backward(1, s) for s in outward[:2]}
            collects[0].receive(order, "first_low", "second_high")
            collects[0].near(order)
            if pieces == 2:
                for s in outward[2:-1]:
                    parts[s] = backward(1, s)

        with jax.named_scope("middle_norm"):
            back2_pre, gg2_pre = norm_back(order(gn2).astype(F32), middle_pre, inv2_pre, gain2_pre)
            resid_pre = g_pre.astype(F32) + back2_pre
            gb_pre = everyones(order(resid_pre.astype(BF)), k)
            if pieces == 2:
                parts[0] = backward(1, 0)
            back = [collects[0].result(order).reshape(n, depth, 3 * sizes[0])]
            gw_act = jnp.concatenate([mm_tn(nall_act, grad), mm_tn(gall_act, hidden)], axis=1)
            gw_act = gw_act.astype(BF).reshape(n, adepth, 3 * aunits)
            back[0] = exchange(order(jnp.concatenate([back[0], beside(gw_act, sizes[0])], axis=1)))
            for s in parts:
                collects[1].put(s, order(parts[s]))

            gn2_act, out_act = total(gn2_act), total(out_act)
            output_act = (
                lax.dynamic_slice_in_dim(middle_act, mine * awide, awide, 1) + out_act
            )[:arows]
            back2_act, gg2_act = norm_back(order(gn2_act), middle_act, inv2_act, gain2_act)
            resid_act = g_act.astype(F32) + back2_act
            gb_act = resid_act.astype(BF)
            gm_act = order(mm(gb_act, wout_act).astype(BF))
            start = jnp.zeros((padded + apad, 2 * HD), F32)
            gq_act, start = order(
                *attend_back(
                    camera_counts, text_lengths, q_act, gm_act, kv_all, start, F32,
                    heads, padded, arows, 1, padded + apad,
                )
            )
            gb_pre = placed(order(*gb_pre), mine, 0)
        with jax.named_scope("attention_back"):
            gm_pre = order(mm(gb_pre, wout_pre).astype(BF))
            gq_pre, gkv = order(
                *attend_back(
                    camera_counts, text_lengths, qkv_p, gm_pre, kv_p, start, BF,
                    heads, padded, 0, tiles, padded,
                )
            )
            gkv = handed(gkv, mine, k, 1)
            if pieces == 2:
                collects[1].far(order)
                collects[1].near(order)
            back[0] = order(back[0])
            go = order(pair_grad(gb_pre, mixed_pre, gb_act, mixed_act, n)).reshape(-1, qcols)
            go = lax.psum_scatter(go, "dp", scatter_dimension=0, tiled=True)
            gkv = total(order(*gkv)).astype(BF)
            gqkv_pre = order(jnp.concatenate([gq_pre, gkv[:padded]], axis=1))
            gqkv_act = jnp.concatenate([gq_act, gkv[padded:]], axis=1)
            gn_pre = order(mm_nt(gqkv_pre, wqkv_pre).astype(BF))
            gn_pre = handed(gn_pre, mine, k, 0)
            gn_act = (mm_nt(gq_act, wq_act) + mm_nt(gkv[padded:], wkv_act)).astype(BF)
            gn_act = everyones(order(gn_act), k)

        with jax.named_scope("query_key_value_grads"):
            gw = order(pair_grad(order(normed_pre), gqkv_pre, normed_act, gqkv_act, n))
            gw = gw.reshape(-1, qcols + kvcols)
            gw = lax.psum_scatter(gw, "dp", scatter_dimension=0, tiled=True)
            if pieces == 2:
                back1 = collects[1].result(order).reshape(n, depth, 3 * sizes[1])
                back.append(exchange(order(back1)))

        with jax.named_scope("input_grads"):
            gn_pre = total(order(*gn_pre))
            invrow = lax.dynamic_slice_in_dim(inv_pre, mine * block, block, 0)
            back_pre, gg_pre = norm_back(gn_pre, xrow_pre, invrow, gain_pre)
            in_pre = order((resid_pre + back_pre).astype(BF))
            in_pre = handed(in_pre, mine, k, 1)
            out_pre = order((middle_pre + order(ffn).astype(F32)).astype(BF))
            out_pre = handed(out_pre, mine, k, 1)
            gn_act = total(order(*gn_act))
            back_act, gg_act = norm_back(gn_act, x_act, inv_act, gain_act)
            in_act = lax.dynamic_slice_in_dim(resid_act + back_act, mine * awide, awide, 1)[:arows]

        with jax.named_scope("gain_grads"):

            def gain_sum(pre, act):
                pre = sum(handed(jnp.stack(pre), mine, k, 1))
                act = lax.dynamic_slice_in_dim(jnp.stack(act), mine * awide, awide, 1)
                both = butterfly_sum(order(jnp.concatenate([pre, act], axis=1)), n)
                return both[0, :wide], both[1, :wide], both[0, wide:], both[1, wide:]

            gg_pre, gg2_pre, gg_act, gg2_act = gain_sum((gg_pre, gg2_pre), (gg_act, gg2_act))

        with jax.named_scope("unit_weight_grads"):
            gw_act = apart(back[0][:, depth:], aunits, adepth)
            gate_act, up_act, down_act = unblock([gw_act])
            in_pre = placed(order(*in_pre), mine, 0)[:rows].astype(F32)
            output_pre = placed(order(*out_pre), mine, 0)[:rows].astype(F32)
            go = order(go).astype(F32)
            gw = order(gw).astype(F32)
            if pieces == 2:
                back[1] = order(back[1])
            gate_pre, up_pre, down_pre = unblock(back, depth)
            gg_pre = gg_pre + order.token[0, 0]
        return (
            output_pre,
            output_act,
            in_pre,
            in_act,
            gg_pre,
            gw[:depth, :qcols],
            gw[:depth, qcols:],
            go[:depth].T,
            gg2_pre,
            gate_pre,
            up_pre,
            down_pre,
            gg_act,
            gw[depth:, :qcols],
            gw[depth:, qcols:],
            go[depth:].T,
            gg2_act,
            gate_act,
            up_act,
            down_act,
        )

    split, rowsplit, whole = P("dp", "mp"), P("mp", "dp"), P("mp")
    weights = (whole, split, split, rowsplit, whole, split, split, rowsplit)
    return jax.shard_map(
        per_device,
        mesh=mesh,
        in_specs=(split, split, P("dp"), P("dp")) + weights + weights + (split, split),
        out_specs=(split, split, split, split) + weights + weights,
        check_vma=False,
    )
```

```python
import functools

import jax
import jax.numpy as jnp
from jax import lax
from jax.experimental import pallas as pl
from jax.experimental.pallas import tpu as pltpu
from jax.sharding import PartitionSpec as P

HD = 256
IMG = 256
CAMS = 3
EPSILON = 1e-06
MASKED = -1e30
BF = jnp.bfloat16
F32 = jnp.float32
SLOPE = 0.7978845608028654
CUBE = 0.044715
VMEM = 56 * 2**20
BRIEF = pl.CostEstimate(flops=1, bytes_accessed=1, transcendentals=0)


def dot(a, b, over_a, over_b):
    return lax.dot_general(a, b, (((over_a,), (over_b,)), ((), ())), preferred_element_type=F32)


def mm(a, b):
    return dot(a, b, 1, 0)


def mm_tn(a, b):
    return dot(a, b, 0, 0)


def mm_nt(a, b):
    return dot(a, b, 1, 1)


def gelu_parts(gate, up, grad_hidden):
    square = gate * gate
    tanh = jnp.tanh(SLOPE * gate * (1.0 + CUBE * square))
    half = 0.5 * (1.0 + tanh)
    act = gate * half
    slope = half + 0.5 * gate * (1.0 - tanh * tanh) * (SLOPE * (1.0 + 3.0 * CUBE * square))
    return act * up, grad_hidden * up * slope, grad_hidden * act


def geglu_kernel(n_ref, g_ref, gate_up_ref, down_ref, hidden_ref, grad_ref):
    units = down_ref.shape[1]
    rows = n_ref.shape[0] * n_ref.shape[1]
    width = n_ref.shape[2]
    both = mm(n_ref[...].reshape(rows, width), gate_up_ref[...])
    grad_hidden = mm(g_ref[...].reshape(rows, width), down_ref[...])
    hidden, grad_gate, grad_up = gelu_parts(both[:, :units], both[:, units:], grad_hidden)
    hidden_ref[...] = hidden.astype(BF)
    grad_ref[:, :units] = grad_gate.astype(BF)
    grad_ref[:, units:] = grad_up.astype(BF)


def geglu(normed, cots, weights, block, step=2):
    n, _, width = normed.shape
    units = weights.shape[1] // 3
    rows = step * block
    return pl.pallas_call(
        geglu_kernel,
        grid=(n // step,),
        in_specs=[
            pl.BlockSpec((step, block, width), lambda i: (i, 0, 0)),
            pl.BlockSpec((step, block, width), lambda i: (i, 0, 0)),
            pl.BlockSpec((width, 2 * units), lambda i: (0, 0)),
            pl.BlockSpec((width, units), lambda i: (0, 2)),
        ],
        out_specs=[
            pl.BlockSpec((rows, units), lambda i: (i, 0)),
            pl.BlockSpec((rows, 2 * units), lambda i: (i, 0)),
        ],
        out_shape=[
            jax.ShapeDtypeStruct((n * block, units), BF),
            jax.ShapeDtypeStruct((n * block, 2 * units), BF),
        ],
        compiler_params=pltpu.CompilerParams(vmem_limit_bytes=VMEM),
        cost_estimate=BRIEF,
        name="geglu",
    )(normed, cots, weights, weights)


def contract_kernel(count, *refs):
    out = refs[-1]
    total = mm_nt(refs[0][...], refs[count][...])
    for s in range(1, count):
        total += mm_nt(refs[s][...], refs[count + s][...])
    if len(refs) > 2 * count + 1:
        total += refs[2 * count][...]
    out[...] = total.astype(out.dtype)


def contract(parts, weights, column, tile, cols, base=None, kind=BF):
    count, rows = len(parts), parts[0].shape[0]
    width = weights[0].shape[0]
    bases = [] if base is None else [base]
    return pl.pallas_call(
        functools.partial(contract_kernel, count),
        grid=(width // cols, rows // tile),
        in_specs=[pl.BlockSpec((tile, part.shape[1]), lambda j, i: (i, 0)) for part in parts]
        + [pl.BlockSpec((cols, part.shape[1]), lambda j, i: (j, column)) for part in parts]
        + [pl.BlockSpec((tile, cols), lambda j, i: (i, j))] * len(bases),
        out_specs=pl.BlockSpec((tile, cols), lambda j, i: (i, j)),
        out_shape=jax.ShapeDtypeStruct((rows, width), kind),
        compiler_params=pltpu.CompilerParams(vmem_limit_bytes=VMEM),
        cost_estimate=BRIEF,
        name="contract",
    )(*parts, *weights, *bases)


def weight_grad_kernel(n_ref, g_ref, grad_ref, hidden_ref, out_ref):
    rows, cols = n_ref.shape[0] * n_ref.shape[1], n_ref.shape[2]
    units = hidden_ref.shape[1]
    out_ref[:, : 2 * units] = mm_tn(n_ref[...].reshape(rows, cols), grad_ref[...]).astype(BF)
    out_ref[:, 2 * units :] = mm_tn(g_ref[...].reshape(rows, cols), hidden_ref[...]).astype(BF)


def weight_grad(normed, cots, grad, hidden, block, cols=1024):
    n, _, width = normed.shape
    units = hidden.shape[1]
    rows = n * block
    return pl.pallas_call(
        weight_grad_kernel,
        grid=(width // cols,),
        in_specs=[
            pl.BlockSpec((n, block, cols), lambda i: (0, 0, i)),
            pl.BlockSpec((n, block, cols), lambda i: (0, 0, i)),
            pl.BlockSpec((rows, 2 * units), lambda i: (0, 0)),
            pl.BlockSpec((rows, units), lambda i: (0, 0)),
        ],
        out_specs=pl.BlockSpec((cols, 3 * units), lambda i: (i, 0)),
        out_shape=jax.ShapeDtypeStruct((width, 3 * units), BF),
        compiler_params=pltpu.CompilerParams(vmem_limit_bytes=VMEM),
        cost_estimate=BRIEF,
        name="weight_grad",
    )(normed, cots, grad, hidden)


def pad_rows(a, rows):
    return jnp.pad(a, ((0, rows - a.shape[0]), (0, 0)))


def swap(a, axis, size, step):
    return lax.ppermute(a, axis, [(i, i ^ step) for i in range(size)])


def exchange(a):
    return lax.all_to_all(a, "dp", 0, 0, tiled=True)


def everyones(a, k):
    return [a] + [swap(a, "mp", k, s) for s in range(1, k)]


def placed(parts, mine, axis):
    size = parts[0].shape[axis]
    shape = list(parts[0].shape)
    shape[axis] *= len(parts)
    whole = jnp.zeros(shape, parts[0].dtype)
    for s, part in enumerate(parts):
        whole = lax.dynamic_update_slice_in_dim(whole, part, (mine ^ s) * size, axis)
    return whole


def handed(a, mine, k, axis):
    size = a.shape[axis] // k
    cut = [lax.dynamic_slice_in_dim(a, (mine ^ s) * size, size, axis) for s in range(k)]
    return [cut[0]] + [swap(cut[s], "mp", k, s) for s in range(1, k)]


def total(parts):
    return sum(part.astype(F32) for part in parts)


def butterfly_sum(a, n):
    step = 1
    while step < n:
        a = a + swap(a, "dp", n, step)
        step *= 2
    return a


class Halving:
    def __init__(self, a, n, me):
        self.a, self.n, self.me, self.step = a, n, me, 1
        self.send()

    def send(self):
        if self.step == self.n:
            return
        a = self.a
        pairs = a.reshape((a.shape[0] // 2, 2) + a.shape[1:])
        bit = (self.me // self.step) % 2
        self.keep = lax.dynamic_index_in_dim(pairs, bit, 1, keepdims=False)
        send = lax.dynamic_index_in_dim(pairs, 1 - bit, 1, keepdims=False)
        self.got = swap(send, "dp", self.n, self.step)

    def take(self, order):
        if self.step == self.n:
            return
        self.a = (self.keep.astype(F32) + order(self.got).astype(F32)).astype(BF)
        self.step *= 2
        self.send()

    def result(self, order):
        while self.step < self.n:
            self.take(order)
        return self.a[0]


class Spread:
    def __init__(self, block, k):
        self.k = k
        if k == 4:
            self.blocks = [block, swap(block, "mp", k, 1), swap(block, "mp", k, 2)]
        else:
            self.blocks = everyones(block, k)

    def arrive(self, order):
        self.blocks[1:] = order(*self.blocks[1:])
        if self.k == 4:
            half = self.blocks[0].shape[0] // 2
            self.low = swap(self.blocks[2][:half], "mp", 4, 1)
            self.high = swap(self.blocks[1][half:], "mp", 4, 2)

    def last(self, order):
        if self.k == 4:
            self.blocks.append(order(jnp.concatenate(order(self.low, self.high), axis=0)))


class Collect:
    def __init__(self, k):
        self.k, self.parts, self.got = k, {}, {}

    def put(self, s, part):
        self.parts[s] = part
        half = part.shape[0] // 2
        if self.k != 4:
            if s:
                self.got[s] = swap(part, "mp", self.k, s)
        elif s == 3:
            self.low = swap(part[:half], "mp", 4, 1)
            self.high = swap(part[half:], "mp", 4, 2)
        elif s == 1:
            self.got["first_low"] = swap(part[:half], "mp", 4, 1)
        elif s == 2:
            self.got["second_high"] = swap(part[half:], "mp", 4, 2)

    def receive(self, order, *names):
        for name in names:
            if name in self.got:
                self.got[name] = order(self.got[name])

    def far(self, order):
        if self.k == 4:
            self.low, self.high = order(self.low, self.high)

    def near(self, order):
        if self.k == 4:
            half = self.low.shape[0]
            low, high = order(
                total([self.parts[2][:half], self.low]).astype(BF),
                total([self.parts[1][half:], self.high]).astype(BF),
            )
            self.got["second_low"] = swap(low, "mp", 4, 2)
            self.got["first_high"] = swap(high, "mp", 4, 1)

    def result(self, order):
        own, got = self.parts[0], self.got
        if self.k != 4:
            return order(total([own, *order(*got.values())]).astype(BF))
        self.receive(order, "first_low", "second_high", "second_low", "first_high")
        half = self.low.shape[0]
        lower = total([own[:half], got["first_low"], got["second_low"]]).astype(BF)
        upper = total([own[half:], got["second_high"], got["first_high"]]).astype(BF)
        return order(jnp.concatenate([lower, upper], axis=0))


def inverse_rms(x):
    return lax.rsqrt(jnp.mean(x * x, axis=1, keepdims=True) + EPSILON)


def norm_back(grad, x, inv, gain):
    inner = jnp.sum(grad * gain * x, axis=1, keepdims=True)
    back = inv * gain * grad - x * inv**3 * inner / x.shape[1]
    return back, jnp.sum(grad * x * inv, axis=0)


def key_weights(queries, keys, cameras, texts, padded, tail):
    scores = mm_nt(queries, keys) * HD ** (-0.5)
    place = lax.broadcasted_iota(jnp.int32, scores.shape, 1)
    text = CAMS * IMG
    seen = (place < cameras * IMG) | ((place >= text) & (place < text + texts))
    if keys.shape[0] > padded:
        seen = seen | ((place >= padded) & (place < padded + tail))
    scores = jnp.where(seen, scores, MASKED)
    terms = jnp.exp(scores - jnp.max(scores, axis=1, keepdims=True))
    return terms / jnp.sum(terms, axis=1, keepdims=True)


def attend_kernel(padded, tail, cams_ref, texts_ref, q_ref, k_ref, v_ref, mixed_ref):
    weights = key_weights(q_ref[...], k_ref[...], cams_ref[0], texts_ref[0], padded, tail)
    mixed_ref[...] = mm(weights.astype(BF), v_ref[...]).astype(BF)


def attend(cameras, texts, queries, kv, heads, padded, tail, tiles):
    rows, keys = queries.shape[0], kv.shape[0]
    tile = rows // tiles
    return pl.pallas_call(
        functools.partial(attend_kernel, padded, tail),
        grid=(heads, tiles),
        in_specs=[
            pl.BlockSpec(memory_space=pltpu.SMEM),
            pl.BlockSpec(memory_space=pltpu.SMEM),
            pl.BlockSpec((tile, HD), lambda h, i: (i, h)),
            pl.BlockSpec((keys, HD), lambda h, i: (0, 0)),
            pl.BlockSpec((keys, HD), lambda h, i: (0, 1)),
        ],
        out_specs=pl.BlockSpec((tile, HD), lambda h, i: (i, h)),
        out_shape=jax.ShapeDtypeStruct((rows, heads * HD), BF),
        compiler_params=pltpu.CompilerParams(vmem_limit_bytes=VMEM),
        cost_estimate=BRIEF,
        name="attend",
    )(cameras, texts, queries, kv, kv)


def attend_back_kernel(
    padded, tail, cams_ref, texts_ref, q_ref, gm_ref, k_ref, v_ref, start_ref, gq_ref, gkv_ref, sum_ref
):
    first = (pl.program_id(0) == 0) & (pl.program_id(1) == 0)
    last = (pl.program_id(0) == pl.num_programs(0) - 1) & (
        pl.program_id(1) == pl.num_programs(1) - 1
    )
    keys = k_ref.shape[0]

    @pl.when(first)
    def _():
        sum_ref[...] = start_ref[...]

    queries, grad_mixed = q_ref[...], gm_ref[...]
    weights = key_weights(queries, k_ref[...], cams_ref[0], texts_ref[0], padded, tail)
    grad = mm_nt(grad_mixed, v_ref[...])
    inner = jnp.sum(weights * grad, axis=1, keepdims=True)
    grad = (weights * (grad - inner)).astype(BF)
    gq_ref[...] = (mm(grad, k_ref[...]) * HD ** (-0.5)).astype(BF)
    sum_ref[:keys, :HD] += mm_tn(grad, queries) * HD ** (-0.5)
    sum_ref[:keys, HD:] += mm_tn(weights.astype(BF), grad_mixed)

    @pl.when(last)
    def _():
        gkv_ref[...] = sum_ref[...].astype(gkv_ref.dtype)


def attend_back(cameras, texts, queries, grad_mixed, kv, start, kind, heads, padded, tail, tiles, keys):
    rows = queries.shape[0]
    tile = rows // tiles
    return pl.pallas_call(
        functools.partial(attend_back_kernel, padded, tail),
        grid=(heads, tiles),
        in_specs=[
            pl.BlockSpec(memory_space=pltpu.SMEM),
            pl.BlockSpec(memory_space=pltpu.SMEM),
            pl.BlockSpec((tile, HD), lambda h, i: (i, h)),
            pl.BlockSpec((tile, HD), lambda h, i: (i, h)),
            pl.BlockSpec((keys, HD), lambda h, i: (0, 0)),
            pl.BlockSpec((keys, HD), lambda h, i: (0, 1)),
            pl.BlockSpec(start.shape, lambda h, i: (0, 0)),
        ],
        out_specs=[
            pl.BlockSpec((tile, HD), lambda h, i: (i, h)),
            pl.BlockSpec(start.shape, lambda h, i: (0, 0)),
        ],
        out_shape=[
            jax.ShapeDtypeStruct((rows, heads * HD), BF),
            jax.ShapeDtypeStruct(start.shape, kind),
        ],
        scratch_shapes=[pltpu.VMEM(start.shape, F32)],
        compiler_params=pltpu.CompilerParams(vmem_limit_bytes=VMEM),
        cost_estimate=BRIEF,
        name="attend_back",
    )(cameras, texts, queries, grad_mixed, kv, kv, start)


def pair_grad_kernel(pre_ref, by_pre_ref, act_ref, by_act_ref, out_ref):
    depth = pre_ref.shape[1]
    out_ref[0, :depth] = mm_tn(pre_ref[...], by_pre_ref[...]).astype(BF)
    act = act_ref[...] if len(act_ref.shape) == 2 else act_ref[0]
    out_ref[0, depth:] = mm_tn(act, by_act_ref[...]).astype(BF)


def pair_grad(pre, by_pre, act, by_act, n):
    depth, adepth, cols = pre.shape[1] // n, act.shape[1] // n, by_pre.shape[1]
    act_spec = pl.BlockSpec((act.shape[0], adepth), lambda i: (0, i))
    if adepth % 128:
        act = act.reshape(-1, n, adepth).transpose(1, 0, 2)
        act_spec = pl.BlockSpec((1,) + act.shape[1:], lambda i: (i, 0, 0))
    return pl.pallas_call(
        pair_grad_kernel,
        grid=(n,),
        in_specs=[
            pl.BlockSpec((pre.shape[0], depth), lambda i: (0, i)),
            pl.BlockSpec(by_pre.shape, lambda i: (0, 0)),
            act_spec,
            pl.BlockSpec(by_act.shape, lambda i: (0, 0)),
        ],
        out_specs=pl.BlockSpec((1, depth + adepth, cols), lambda i: (i, 0, 0)),
        out_shape=jax.ShapeDtypeStruct((n, depth + adepth, cols), BF),
        compiler_params=pltpu.CompilerParams(vmem_limit_bytes=VMEM),
        cost_estimate=BRIEF,
        name="pair_grad",
    )(pre, by_pre, act, by_act)


def cuts_of(sizes):
    at = 0
    for size in sizes:
        yield slice(at, at + size)
        at += size


def pack_kernel(sizes, gate_ref, up_ref, down_ref, *outs):
    for units, cut, out in zip(sizes, cuts_of(sizes), outs):
        out[0, :, :units] = gate_ref[:, cut]
        out[0, :, units : 2 * units] = up_ref[:, cut]
        out[0, :, 2 * units :] = down_ref[cut, :].astype(F32).T.astype(BF)


def unit_blocks(gate, up, down, n, sizes):
    depth, block = gate.shape[0], gate.shape[1] // n
    if block % 128:
        return [
            jnp.concatenate(
                [
                    gate.reshape(depth, n, block).transpose(1, 0, 2),
                    up.reshape(depth, n, block).transpose(1, 0, 2),
                    down.reshape(n, block, depth).transpose(0, 2, 1),
                ],
                axis=2,
            )
        ]
    return pl.pallas_call(
        functools.partial(pack_kernel, sizes),
        grid=(n,),
        in_specs=[
            pl.BlockSpec((depth, block), lambda i: (0, i)),
            pl.BlockSpec((depth, block), lambda i: (0, i)),
            pl.BlockSpec((block, depth), lambda i: (i, 0)),
        ],
        out_specs=[pl.BlockSpec((1, depth, 3 * units), lambda i: (i, 0, 0)) for units in sizes],
        out_shape=[jax.ShapeDtypeStruct((n, depth, 3 * units), BF) for units in sizes],
        compiler_params=pltpu.CompilerParams(vmem_limit_bytes=VMEM),
        cost_estimate=BRIEF,
        name="pack",
    )(gate, up, down)


def beside(blocks, units):
    n, rows, cols = blocks.shape
    groups = 3 * units // cols
    each = -(-rows // (16 * groups)) * 16
    blocks = jnp.pad(blocks, ((0, 0), (0, each * groups - rows), (0, 0)))
    return jnp.concatenate(jnp.split(blocks, groups, axis=1), axis=2)


def apart(blocks, units, rows):
    groups = blocks.shape[2] // (3 * units)
    return jnp.concatenate(jnp.split(blocks, groups, axis=2), axis=1)[:, :rows]


def unpack_kernel(*refs):
    parts, (gate_ref, up_ref, down_ref) = refs[:-3], refs[-3:]
    sizes = [part.shape[2] // 3 for part in parts]
    for units, cut, part in zip(sizes, cuts_of(sizes), parts):
        gate_ref[:, cut] = part[0, :, :units].astype(F32)
        up_ref[:, cut] = part[0, :, units : 2 * units].astype(F32)
        down_ref[cut, :] = part[0, :, 2 * units :].astype(F32).T


def unblock(parts, depth=None):
    n = parts[0].shape[0]
    depth = depth or parts[0].shape[1]
    block = sum(part.shape[2] // 3 for part in parts)
    if block % 128:
        part = parts[0][:, :depth]
        gate = part[:, :, :block].transpose(1, 0, 2).reshape(depth, n * block)
        up = part[:, :, block : 2 * block].transpose(1, 0, 2).reshape(depth, n * block)
        down = part[:, :, 2 * block :].transpose(0, 2, 1).reshape(n * block, depth)
        return gate.astype(F32), up.astype(F32), down.astype(F32)
    return pl.pallas_call(
        unpack_kernel,
        grid=(n,),
        in_specs=[
            pl.BlockSpec((1, depth, part.shape[2]), lambda i: (i, 0, 0)) for part in parts
        ],
        out_specs=[
            pl.BlockSpec((depth, block), lambda i: (0, i)),
            pl.BlockSpec((depth, block), lambda i: (0, i)),
            pl.BlockSpec((block, depth), lambda i: (i, 0)),
        ],
        out_shape=[
            jax.ShapeDtypeStruct((depth, n * block), F32),
            jax.ShapeDtypeStruct((depth, n * block), F32),
            jax.ShapeDtypeStruct((n * block, depth), F32),
        ],
        compiler_params=pltpu.CompilerParams(vmem_limit_bytes=VMEM),
        cost_estimate=BRIEF,
        name="unpack",
    )(*parts)


class Order:
    def __init__(self):
        self.token = jnp.zeros((8, 128), F32)

    def __call__(self, *values):
        *values, self.token = lax.optimization_barrier(values + (self.token,))
        return values[0] if len(values) == 1 else tuple(values)


def solution(mesh):
    n, k = mesh.shape["dp"], mesh.shape["mp"]

    def per_device(
        prefix_tokens,
        action_tokens,
        camera_counts,
        text_lengths,
        prefix_attn_gain,
        prefix_query_proj,
        prefix_kv_proj,
        prefix_out_proj,
        prefix_ffn_gain,
        prefix_gate_proj,
        prefix_up_proj,
        prefix_down_proj,
        action_attn_gain,
        action_query_proj,
        action_kv_proj,
        action_out_proj,
        action_ffn_gain,
        action_gate_proj,
        action_up_proj,
        action_down_proj,
        prefix_cotangent,
        action_cotangent,
    ):
        mine, me = lax.axis_index("mp"), lax.axis_index("dp")
        rows, wide = prefix_tokens.shape
        arows, awide = action_tokens.shape
        block = -(-rows // (16 * k)) * 16
        padded = block * k
        apad = -(-arows // 64) * 64
        width, awidth = wide * k, awide * k
        fold = apad * awidth // width
        heads = prefix_query_proj.shape[1] // HD
        qcols = heads * HD
        kvcols = prefix_kv_proj.shape[1]
        depth, adepth = prefix_query_proj.shape[0], action_query_proj.shape[0]
        units = prefix_gate_proj.shape[1] // n
        sizes = [units // 2] * 2 if units % 256 == 0 else [units]
        pieces = len(sizes)

        order = Order()

        with jax.named_scope("token_features"):
            x_act = pad_rows(action_tokens, apad)
            x_all = jnp.concatenate(
                [pad_rows(prefix_tokens, padded), x_act.reshape(-1, wide)], axis=0
            )
            x_all = everyones(order(x_all), k)
            gains = jnp.concatenate(
                [prefix_attn_gain, prefix_ffn_gain, action_attn_gain, action_ffn_gain]
            )[None]
            gains = everyones(gains, k)

        with jax.named_scope("cotangents"):
            g_act = everyones(pad_rows(action_cotangent, apad), k)
            g_pre = handed(pad_rows(prefix_cotangent, padded), mine, k, 0)

        with jax.named_scope("attention_weights"):
            qkv_pre = jnp.concatenate([prefix_query_proj, prefix_kv_proj], axis=1)
            wqkv_pre = lax.all_gather(order(qkv_pre), "dp", axis=0, tiled=True)
            group = qcols // kvcols
            wout_pre = lax.all_gather(order(prefix_out_proj.T), "dp", axis=0, tiled=True)
            rest = jnp.concatenate(
                [action_out_proj.T, action_query_proj]
                + [jnp.concatenate(jnp.split(action_kv_proj, group, axis=0), axis=1)],
                axis=0,
            )

        with jax.named_scope("unit_weights"):
            packed = list(
                unit_blocks(prefix_gate_proj, prefix_up_proj, prefix_down_proj, n, sizes)
            )
            own = [exchange(order(packed[0])).reshape(width, 3 * sizes[0])]

        with jax.named_scope("token_features"):
            g_pre = placed(order(*g_pre), mine, 1)
            g_act = placed(order(*g_act), mine, 1)
            g_rows = order(jnp.concatenate([g_pre, g_act.reshape(fold, width)], axis=0))
            gall = lax.all_gather(g_rows, "dp", axis=0)
            gains = placed(order(*gains), mine, 0)
            gain_pre = gains[:, :wide].reshape(1, width)
            gain2_pre = gains[:, wide : 2 * wide].reshape(1, width)
            gain_act = gains[:, 2 * wide : 2 * wide + awide].reshape(1, awidth)
            gain2_act = gains[:, 2 * wide + awide :].reshape(1, awidth)
            x_all = order(*x_all)
            x_pre = order(placed([x[:padded] for x in x_all], mine, 1)).astype(F32)
            x_act = placed([x[padded:].reshape(apad, awide) for x in x_all], mine, 1).astype(F32)

        with jax.named_scope("attention"):
            inv_pre = inverse_rms(x_pre)
            normed_pre = order((x_pre * inv_pre * gain_pre).astype(BF))
            qkv_p = order(mm(normed_pre, order(wqkv_pre)).astype(BF))
            kv_p = everyones(qkv_p[:, qcols:], k)
            kv_p = placed(order(*kv_p), mine, 1)
            tiles = k
            mixed_pre = order(
                attend(camera_counts, text_lengths, qkv_p, kv_p, heads, padded, 0, tiles)
            )
            own[0] = order(own[0])
            branch_pre = order(mm_nt(mixed_pre, order(wout_pre)).astype(BF))
            branch_pre = handed(branch_pre, mine, k, 0)

            xrow_pre = lax.dynamic_slice_in_dim(x_pre, mine * block, block, 0)
            middle_pre = xrow_pre + total(order(*branch_pre))
            inv2_pre = inverse_rms(middle_pre)
            normed2_pre = order((middle_pre * inv2_pre * gain2_pre).astype(BF))
            nall = lax.all_gather(normed2_pre, "dp", axis=0)

            spread = [Spread(order(own[0]), k)]
            aunits = action_gate_proj.shape[1] // n
            [w_act] = unit_blocks(action_gate_proj, action_up_proj, action_down_proj, n, [aunits])
            w_act = exchange(order(w_act))
            rest = lax.all_gather(order(rest), "dp", axis=0)
            spread[0].arrive(order)

        with jax.named_scope("geglu"):
            w_act = order(w_act).reshape(awidth, 3 * aunits)
            gu_act, dt_act = w_act[:, : 2 * aunits], w_act[:, 2 * aunits :]
            gall, nall = order(gall, nall)
            if pieces == 2:
                own.append(exchange(order(packed[1])).reshape(width, 3 * sizes[1]))
            hiddens = [[None] * k for _ in range(pieces)]
            grads = [[None] * k for _ in range(pieces)]
            collects = [Collect(k) for _ in range(pieces)]
            outward = list(range(k - 1, -1, -1))

            def forward(c, s):
                hidden, grad = geglu(order(nall), gall, spread[c].blocks[s], block)
                hiddens[c][s], grads[c][s] = order(hidden, grad)

            def backward(c, s):
                part = weight_grad(order(nall), gall, grads[c][s], hiddens[c][s], block)
                return order(part)

            for s in range(k if k != 4 else 3):
                forward(0, s)
            spread[0].last(order)
            if k == 4:
                forward(0, 3)

            rest = order(rest)
            wout_act = rest[:, :adepth].reshape(n * adepth, qcols)
            wq_act = rest[:, adepth : 2 * adepth].reshape(n * adepth, qcols)
            wkv_act = jnp.concatenate(
                jnp.split(rest[:, 2 * adepth :], group, axis=2), axis=1
            ).reshape(n * adepth, kvcols)
            inv_act = inverse_rms(x_act)
            normed_act = (x_act * inv_act * gain_act).astype(BF)
            q_act, kv_a = order(mm(normed_act, wq_act).astype(BF), mm(normed_act, wkv_act).astype(BF))
            kv_a = everyones(kv_a, k)
            parts = [None] * k
            parts[1] = backward(0, 1)
            kv_a = placed(order(*kv_a), mine, 1)
            kv_all = order(jnp.concatenate([kv_p, kv_a], axis=0))
            mixed_act = order(
                attend(camera_counts, text_lengths, q_act, kv_all, heads, padded, arows, 1)
            )
            branch_act = everyones(order(mm_nt(mixed_act, wout_act).astype(BF)), k)
            parts[2] = backward(0, 2)
            middle_act = x_act + total(order(*branch_act))
            inv2_act = inverse_rms(middle_act)
            normed2_act = order((middle_act * inv2_act * gain2_act).astype(BF))
            nall_act = lax.all_gather(normed2_act, "dp", axis=0, tiled=True)
            if pieces == 2:
                own[1] = order(own[1])
                spread.append(Spread(own[1], k))
            parts[0] = backward(0, 0)
            if pieces == 2:
                forward(1, 0)

            gall_act = gall[:, block:].reshape(n * apad, awidth)
            both = mm(order(nall_act), gu_act)
            hidden, grad_gate, grad_up = gelu_parts(
                both[:, :aunits], both[:, aunits:], mm(gall_act, dt_act)
            )
            hidden = hidden.astype(BF)
            grad = jnp.concatenate([grad_gate, grad_up], axis=1).astype(BF)
            part = jnp.concatenate([mm_nt(hidden, dt_act), mm_nt(grad, gu_act)], axis=1).astype(BF)
            part = order(part)

            halving = Halving(part.reshape(n, apad, 2 * awidth), n, me)

            tile = n * block // 4
            gn2 = ffn = None
            if pieces == 2:
                gn2 = order(
                    contract([order(grads[0][0])] + grads[0][1:], spread[0].blocks, 0, tile, 1024, None, F32)
                )
            halving.take(order)
            for s in range(3, k):
                parts[s] = backward(0, s)
            halving.take(order)
            if pieces == 2:
                spread[1].arrive(order)
                forward(1, 1)
            halving.take(order)
            part = halving.result(order)
            out_act = handed(part[:, :awidth], mine, k, 1)
            gn2_act = everyones(part[:, awidth:], k)
            if pieces == 2:
                for s in range(2, k if k != 4 else 3):
                    forward(1, s)
                spread[1].last(order)
                if k == 4:
                    forward(1, 3)
            gn2_act, out_act = order(*gn2_act), order(*out_act)
            for s in outward:
                collects[0].put(s, order(parts[s]))
            last = pieces - 1
            gn2 = order(
                contract([order(grads[last][0])] + grads[last][1:], spread[last].blocks, 0, tile, 1024, gn2)
            )
            gn2 = lax.psum_scatter(gn2, "dp", scatter_dimension=0, tiled=True)
            collects[0].far(order)
            flat = [weights for piece in spread for weights in piece.blocks]
            flat_hiddens = [hidden for piece in hiddens for hidden in piece]
            ffn = order(contract([order(flat_hiddens[0])] + flat_hiddens[1:], flat, 2, tile, 1024))
            ffn = lax.psum_scatter(ffn, "dp", scatter_dimension=0, tiled=True)
            parts = {}
            if pieces == 2:
                parts = {s: backward(1, s) for s in outward[:2]}
            collects[0].receive(order, "first_low", "second_high")
            collects[0].near(order)
            if pieces == 2:
                for s in outward[2:-1]:
                    parts[s] = backward(1, s)

        with jax.named_scope("middle_norm"):
            back2_pre, gg2_pre = norm_back(order(gn2).astype(F32), middle_pre, inv2_pre, gain2_pre)
            resid_pre = g_pre.astype(F32) + back2_pre
            gb_pre = everyones(order(resid_pre.astype(BF)), k)
            if pieces == 2:
                parts[0] = backward(1, 0)
            back = [collects[0].result(order).reshape(n, depth, 3 * sizes[0])]
            gw_act = jnp.concatenate([mm_tn(nall_act, grad), mm_tn(gall_act, hidden)], axis=1)
            gw_act = gw_act.astype(BF).reshape(n, adepth, 3 * aunits)
            back[0] = exchange(order(jnp.concatenate([back[0], beside(gw_act, sizes[0])], axis=1)))
            for s in parts:
                collects[1].put(s, order(parts[s]))

            gn2_act, out_act = total(gn2_act), total(out_act)
            output_act = (
                lax.dynamic_slice_in_dim(middle_act, mine * awide, awide, 1) + out_act
            )[:arows]
            back2_act, gg2_act = norm_back(order(gn2_act), middle_act, inv2_act, gain2_act)
            resid_act = g_act.astype(F32) + back2_act
            gb_act = resid_act.astype(BF)
            gm_act = order(mm(gb_act, wout_act).astype(BF))
            start = jnp.zeros((padded + apad, 2 * HD), F32)
            gq_act, start = order(
                *attend_back(
                    camera_counts, text_lengths, q_act, gm_act, kv_all, start, F32,
                    heads, padded, arows, 1, padded + apad,
                )
            )
            gb_pre = placed(order(*gb_pre), mine, 0)
        with jax.named_scope("attention_back"):
            gm_pre = order(mm(gb_pre, wout_pre).astype(BF))
            gq_pre, gkv = order(
                *attend_back(
                    camera_counts, text_lengths, qkv_p, gm_pre, kv_p, start, BF,
                    heads, padded, 0, tiles, padded,
                )
            )
            gkv = handed(gkv, mine, k, 1)
            if pieces == 2:
                collects[1].far(order)
                collects[1].near(order)
            back[0] = order(back[0])
            go = order(pair_grad(gb_pre, mixed_pre, gb_act, mixed_act, n)).reshape(-1, qcols)
            go = lax.psum_scatter(go, "dp", scatter_dimension=0, tiled=True)
            gkv = total(order(*gkv)).astype(BF)
            gqkv_pre = order(jnp.concatenate([gq_pre, gkv[:padded]], axis=1))
            gqkv_act = jnp.concatenate([gq_act, gkv[padded:]], axis=1)
            gn_pre = order(mm_nt(gqkv_pre, wqkv_pre).astype(BF))
            gn_pre = handed(gn_pre, mine, k, 0)
            gn_act = (mm_nt(gq_act, wq_act) + mm_nt(gkv[padded:], wkv_act)).astype(BF)
            gn_act = everyones(order(gn_act), k)

        with jax.named_scope("query_key_value_grads"):
            gw = order(pair_grad(order(normed_pre), gqkv_pre, normed_act, gqkv_act, n))
            gw = gw.reshape(-1, qcols + kvcols)
            gw = lax.psum_scatter(gw, "dp", scatter_dimension=0, tiled=True)
            if pieces == 2:
                back1 = collects[1].result(order).reshape(n, depth, 3 * sizes[1])
                back.append(exchange(order(back1)))

        with jax.named_scope("input_grads"):
            gn_pre = total(order(*gn_pre))
            invrow = lax.dynamic_slice_in_dim(inv_pre, mine * block, block, 0)
            back_pre, gg_pre = norm_back(gn_pre, xrow_pre, invrow, gain_pre)
            in_pre = order((resid_pre + back_pre).astype(BF))
            in_pre = handed(in_pre, mine, k, 1)
            out_pre = order((middle_pre + order(ffn).astype(F32)).astype(BF))
            out_pre = handed(out_pre, mine, k, 1)
            gn_act = total(order(*gn_act))
            back_act, gg_act = norm_back(gn_act, x_act, inv_act, gain_act)
            in_act = lax.dynamic_slice_in_dim(resid_act + back_act, mine * awide, awide, 1)[:arows]

        with jax.named_scope("gain_grads"):

            def gain_sum(pre, act):
                pre = sum(handed(jnp.stack(pre), mine, k, 1))
                act = lax.dynamic_slice_in_dim(jnp.stack(act), mine * awide, awide, 1)
                both = butterfly_sum(order(jnp.concatenate([pre, act], axis=1)), n)
                return both[0, :wide], both[1, :wide], both[0, wide:], both[1, wide:]

            gg_pre, gg2_pre, gg_act, gg2_act = gain_sum((gg_pre, gg2_pre), (gg_act, gg2_act))

        with jax.named_scope("unit_weight_grads"):
            gw_act = apart(back[0][:, depth:], aunits, adepth)
            gate_act, up_act, down_act = unblock([gw_act])
            in_pre = placed(order(*in_pre), mine, 0)[:rows].astype(F32)
            output_pre = placed(order(*out_pre), mine, 0)[:rows].astype(F32)
            go = order(go).astype(F32)
            gw = order(gw).astype(F32)
            if pieces == 2:
                back[1] = order(back[1])
            gate_pre, up_pre, down_pre = unblock(back, depth)
            gg_pre = gg_pre + order.token[0, 0]
        return (
            output_pre,
            output_act,
            in_pre,
            in_act,
            gg_pre,
            gw[:depth, :qcols],
            gw[:depth, qcols:],
            go[:depth].T,
            gg2_pre,
            gate_pre,
            up_pre,
            down_pre,
            gg_act,
            gw[depth:, :qcols],
            gw[depth:, qcols:],
            go[depth:].T,
            gg2_act,
            gate_act,
            up_act,
            down_act,
        )

    split, rowsplit, whole = P("dp", "mp"), P("mp", "dp"), P("mp")
    weights = (whole, split, split, rowsplit, whole, split, split, rowsplit)
    return jax.shard_map(
        per_device,
        mesh=mesh,
        in_specs=(split, split, P("dp"), P("dp")) + weights + weights + (split, split),
        out_specs=(split, split, split, split) + weights + weights,
        check_vma=False,
    )
```
